256 devices in a mesh: dp: 16 (over y_lo, z), mp: 16 (over y_hi, x, core).
Axes of the slice: x: 4, y: 4 (y_hi: 2, y_lo: 2; y = y_hi * 2 + y_lo), z: 8, core: 2. Of those that a mesh axis runs over, the one named last changes fastest.
Arguments:
- inputs: bfloat16 [10240, 1024], P(('dp', 'mp')), may hold values from -24 to 24
- cotangent: bfloat16 [10240, 1024], P(('dp', 'mp')), may hold values from -24 to 24
- segment_ids: int32 [16, 640], P('dp', 'mp'), may hold values from 0 to 7, never falling along the last dimension, each value on 1 to 160 neighbouring positions
- norm_gain: bfloat16 [1024], replicated, may hold values from 0.5 to 1.5
- w_in: bfloat16 [1024, 32768], P(None, 'mp'), may hold values from -0.1875 to 0.1875
- w_out: bfloat16 [32768, 1024], P('mp'), may hold values from -0.03125 to 0.03125
Outputs:
- input_grad: bfloat16 [10240, 1024], P(('dp', 'mp'))
- w_in_grad: bfloat16 [1024, 32768], P('dp', 'mp')
- w_out_grad: bfloat16 [32768, 1024], P('mp', 'dp')
- gain_grad: float32 [1024], replicated
The draws below stay inside these ranges and needn't reach their ends.
Inputs may be any that keep to these rules, and one draw needn't show every extreme that they name: `segment_ids`: within each row the ids never fall and every id appears, each on 1 to 160 tokens, one id on exactly 160; tokens with id 8 - 1 are padding.
All inputs are finite; a program needn't handle non-finite values.
Results may differ from the reference program's by a relative error of at most 0.022.
Values may be sent and summed in bfloat16 or wider, within the bound.
No kernel may reach another device: no remote copies, remote signals or barrier semaphores. Data moves between devices by JAX's collectives and lax.ppermute only.
A program may use at most 128 MiB of HBM per device.

```python
import math
import jax
import jax.numpy as jnp
import numpy as np
from jax import lax

D = 1024
FF = 32768
TOK_GROUP = 640
SEGS = 8
MOST = 160
TOKENS = 10240
N_DP = 16


def raised(values, rng, source, target, shards_of, factor):
    def block_of(axis_at):
        return (jnp.arange(values.shape[axis_at]) // (values.shape[axis_at] // shards_of)).reshape((-1,) + (1,) * (values.ndim - 1 - axis_at))

    one_side = jax.random.permutation(rng, shards_of)[block_of(target)]
    second = (block_of(target) + shards_of // 2) % shards_of
    return jnp.where((block_of(source) == one_side) | (block_of(source) == second), factor * values, values)


def level_of(stream_key, extent, pieces, low, top_value):
    gain = 1.0
    for axis_at, parts in pieces:
        heights = jax.random.uniform(jax.random.fold_in(jax.random.fold_in(stream_key, 6), axis_at), (parts,), jnp.float32, low / len(pieces), top_value / len(pieces))
        gain = gain * jnp.repeat(jnp.exp(heights), extent[axis_at] // parts).reshape((-1,) + (1,) * (len(extent) - 1 - axis_at))
    return gain


def split_up(number_of, total, most, skew):
    portions = [(1 << 20) // math.isqrt(grade ** skew) + 1 for grade in range(2, number_of + 1)]
    rest, holding = total - most - (number_of - 1), [1] * (number_of - 1)
    while rest > 0:
        candidates = [i for i in range(number_of - 1) if holding[i] < most]
        mass, remaining = sum([portions[i] for i in candidates]), rest
        for i in candidates:
            addition = min(most - holding[i], max(1, remaining * portions[i] // mass), rest)
            holding[i] = holding[i] + addition
            rest = rest - addition
    return np.array([most] + holding)


def ragged_sizes(own_key, count, total, reach, lean):
    if count == 2:
        one = jax.random.randint(own_key, (), max(1, total - reach), min(reach, total - 1) + 1)
        return jnp.stack([one, total - one])
    sizes = jnp.asarray(split_up(count, total, reach, lean), jnp.int32)
    twos = (count - 1) // 2
    source_of, sink = sizes[1:1 + 2 * twos:2], sizes[2:2 + 2 * twos:2]
    room = jnp.minimum(source_of - 1, reach - sink)
    shifted = jax.random.randint(jax.random.fold_in(own_key, 1), (twos,), 0, 1 << 20) % (room + 1)
    sizes = sizes.at[1:1 + 2 * twos:2].set(source_of - shifted).at[2:2 + 2 * twos:2].set(sink + shifted)
    return sizes[jax.random.permutation(jax.random.fold_in(own_key, 2), count)]


def bell_draw(key, extent, scale, reach, shards=(), kind=jnp.bfloat16):
    factor_of = level_of(key, extent, shards, -0.22, 0.18) if shards else 1.0
    drawn = jax.random.normal(key, extent, jnp.float32) * scale * factor_of
    return jnp.minimum(jnp.maximum(drawn, -reach), reach).astype(kind)


def heavy_noise(rng, shape, deviation, reach, cuts, heavy, kind=jnp.bfloat16):
    values = deviation * jax.random.normal(rng, shape, jnp.float32)
    if cuts:
        values = values * level_of(rng, shape, cuts, -0.22, 0.18)
    return jnp.clip(raised(values, jax.random.fold_in(rng, 3), *heavy), -reach, reach).astype(kind)


def setup_inputs(seed: int = 0) -> dict:
    arg_keys = jax.random.split(jax.random.key(seed), 7)
    inputs = heavy_noise(arg_keys[0], (TOKENS, D), 1.0, 24.0, ((0, 256),), (0, 1, 256, 6.0))
    cotangent = heavy_noise(arg_keys[1], (TOKENS, D), 1.0, 24.0, ((0, 256),), (0, 1, 256, 6.0))
    segment_ids = jax.vmap(lambda own: jnp.searchsorted(jnp.cumsum(ragged_sizes(own, SEGS, TOK_GROUP, MOST, 2)), jnp.arange(TOK_GROUP), side="right"))(jax.random.split(arg_keys[2], N_DP)).reshape((N_DP, TOK_GROUP)).astype(jnp.int32)
    norm_gain = jnp.clip(1.0 + 0.1 * jax.random.normal(arg_keys[3], (D,), jnp.float32), 0.5, 1.5).astype(jnp.bfloat16)
    w_in = bell_draw(arg_keys[4], (D, FF), D ** -0.5, 0.1875, ((1, 16),))
    w_out = bell_draw(arg_keys[5], (FF, D), FF ** -0.5, 0.03125, ((0, 16),))
    return dict(inputs=inputs, cotangent=cotangent, segment_ids=segment_ids, norm_gain=norm_gain, w_in=w_in, w_out=w_out)


GELU_C = 0.7978845608
GELU_A = 0.044715

def gelu_parts(pre_act):
    inner = jnp.tanh(GELU_C * (pre_act + GELU_A * pre_act * pre_act * pre_act))
    value = 0.5 * pre_act * (1.0 + inner)
    slope = 0.5 * (1.0 + inner) + 0.5 * pre_act * (1.0 - inner * inner) * GELU_C * (1.0 + 3.0 * GELU_A * pre_act * pre_act)
    return (value, slope)

def normalize(values):
    floats = values.astype(jnp.float32)
    inv_rms = lax.rsqrt(lax.optimization_barrier(jnp.mean(floats * floats, axis=-1, keepdims=True)) + 1e-06)
    return (floats * inv_rms, inv_rms)

def token_weights(segment_row):
    labels = jnp.arange(SEGS, dtype=jnp.int32)
    onehot = (segment_row[:, None] == labels[None, :]).astype(jnp.float32)
    counts = lax.optimization_barrier(jnp.sum(onehot, axis=0))
    token_count = lax.optimization_barrier(jnp.sum(onehot * counts[None, :], axis=1))
    weights = jnp.sqrt(TOK_GROUP / (SEGS * token_count))
    return jnp.where(segment_row == SEGS - 1, jnp.zeros_like(weights), weights)

def reference(inputs, cotangent, segment_ids, norm_gain, w_in, w_out):
    grad_scale = 1.0 / math.sqrt(TOKENS)
    gain_f = norm_gain.astype(jnp.float32)
    group_inputs = inputs.reshape(N_DP, TOK_GROUP, D)
    group_cots = cotangent.reshape(N_DP, TOK_GROUP, D)

    def one_group(running, group_item):
        acc_in, acc_out, acc_gain = running
        group_rows, group_cot, segment_row = group_item
        normed, inv_rms = normalize(group_rows)
        xn = (normed * gain_f[None, :]).astype(jnp.bfloat16)
        weights = token_weights(segment_row)
        ge = (group_cot.astype(jnp.float32) * weights[:, None]).astype(jnp.bfloat16)
        pre_act = jnp.dot(xn, w_in, preferred_element_type=jnp.float32)
        act_value, act_slope = gelu_parts(pre_act)
        hidden = act_value.astype(jnp.bfloat16)
        hidden_grad = jnp.dot(ge, w_out.T, preferred_element_type=jnp.float32)
        pre_grad = (hidden_grad * act_slope).astype(jnp.bfloat16)
        normed_raw = jnp.dot(pre_grad, w_in.T, preferred_element_type=jnp.float32)
        normed_grad = normed_raw * gain_f[None, :]
        inner_mean = lax.optimization_barrier(jnp.mean(normed_grad * normed, axis=-1, keepdims=True))
        input_grad = ge.astype(jnp.float32) + inv_rms * (normed_grad - normed * inner_mean)
        part_in = (jnp.dot(xn.T, pre_grad, preferred_element_type=jnp.float32) * grad_scale).astype(jnp.bfloat16)
        part_out = (jnp.dot(ge.T, hidden, preferred_element_type=jnp.float32) * grad_scale).astype(jnp.bfloat16)
        part_in = lax.optimization_barrier(part_in)
        part_out = lax.optimization_barrier(part_out)
        acc_in = acc_in + part_in.astype(jnp.float32)
        acc_out = acc_out + part_out.astype(jnp.float32)
        acc_gain = acc_gain + lax.optimization_barrier(jnp.sum(normed_raw * normed, axis=0))
        return ((acc_in, acc_out, acc_gain), input_grad.astype(jnp.bfloat16))
    start_acc = (jnp.zeros((D, FF), jnp.float32), jnp.zeros((D, FF), jnp.float32), jnp.zeros((D,), jnp.float32))
    final_acc, grads = lax.scan(one_group, start_acc, (group_inputs, group_cots, segment_ids))
    acc_in, acc_out, acc_gain = final_acc
    input_grad = grads.reshape(TOKENS, D)
    return (input_grad, acc_in.astype(jnp.bfloat16), acc_out.T.astype(jnp.bfloat16), acc_gain)
```

```python
import math

import jax
import jax.numpy as jnp
from jax import lax
from jax.sharding import PartitionSpec as P

TOK_GROUP = 640
SEGS = 8
OWN = 40
D = 1024
HID = 1024
AXES = ("dp", "mp")
OFFSETS = (0, 1, -1, 2)

GELU_C = 0.7978845608
GELU_A = 0.044715


def coords(index):
    dp, mp = divmod(index, 16)
    return ((mp // 2) % 4, (mp // 8) * 2 + dp // 8, dp % 8, mp % 2)


def index_of(x, y, z, c):
    x, y, z = x % 4, y % 4, z % 8
    return ((y % 2) * 8 + z) * 16 + ((y // 2) * 4 + x) * 2 + c


def send(value, move):
    pairs = [(i, index_of(*move(*coords(i)))) for i in range(256)]
    return lax.ppermute(value, AXES, pairs)


def first_axis(o):
    return lambda x, y, z, c: (x + o, y, z, c) if c == 0 else (x, y + o, z, c)


def second_axis(o):
    return lambda x, y, z, c: (x, y + o, z, c) if c == 0 else (x + o, y, z, c)


def other_core(x, y, z, c):
    return (x, y, z, 1 - c)


def partner_y(x, y, z, c):
    return (x, y ^ 1, z, c)


def along_z(o):
    return lambda x, y, z, c: (x, y, z + o, c)


def xor_z(o):
    return lambda x, y, z, c: (x, y, z ^ o, c)


def gather_step(block, axis):
    return [block] + [send(block, axis(-o)) for o in OFFSETS[1:]]


def scatter_step(blocks, axis):
    total = blocks[0].astype(jnp.float32)
    for o, block in zip(OFFSETS[1:], blocks[1:]):
        total = total + send(block, axis(o)).astype(jnp.float32)
    return total


def gelu_parts(pre_act):
    inner = jnp.tanh(GELU_C * (pre_act + GELU_A * pre_act * pre_act * pre_act))
    value = 0.5 * pre_act * (1.0 + inner)
    slope = 0.5 * (1.0 + inner) + 0.5 * pre_act * (1.0 - inner * inner) * GELU_C * (
        1.0 + 3.0 * GELU_A * pre_act * pre_act
    )
    return (value, slope)


def weights_of(labels, ids):
    names = jnp.arange(2 * SEGS, dtype=jnp.float32)
    onehot = (labels[:, None] == names[None, :]).astype(jnp.float32)
    counts = jnp.sum(onehot, axis=0)
    token_count = jnp.sum(onehot * counts[None, :], axis=1)
    weights = jnp.sqrt(TOK_GROUP / (SEGS * token_count))
    return jnp.where(ids == SEGS - 1, jnp.zeros_like(weights), weights)


def chain(grad, z, sign, hops):
    def block(k):
        return lax.dynamic_index_in_dim(grad, lax.rem(z + sign * k + 8, 8), 1, False)

    part = block(hops)
    for k in range(hops - 1, 0, -1):
        got = send(part, along_z(sign))
        part = (got.astype(jnp.float32) + block(k).astype(jnp.float32)).astype(jnp.bfloat16)
    return send(part, along_z(sign))


def reduce_z(grad, z, plus_hops, minus_hops):
    grad = grad.reshape(2, 8, 64, HID)
    own = lax.dynamic_index_in_dim(grad, z, 1, False).astype(jnp.float32)
    plus = chain(grad, z, 1, plus_hops)
    minus = chain(grad, z, -1, minus_hops)
    return own + plus.astype(jnp.float32) + minus.astype(jnp.float32)


def join_halves(summed, y_lo):
    summed = summed.astype(jnp.bfloat16)
    mine = lax.dynamic_index_in_dim(summed, y_lo, 0, False)
    give = lax.dynamic_index_in_dim(summed, 1 - y_lo, 0, False)
    got = send(give, partner_y)
    low = jnp.where(y_lo == 0, mine, got)
    high = jnp.where(y_lo == 0, got, mine)
    return jnp.concatenate([low, high], axis=1)


def body(inputs, cotangent, segment_ids, norm_gain, w_in, w_out):
    bf16, f32 = jnp.bfloat16, jnp.float32
    dp = lax.axis_index("dp")
    core = lax.rem(lax.axis_index("mp"), 2)
    y_lo, z = lax.div(dp, 8), lax.rem(dp, 8)
    gain_f = norm_gain.astype(f32)
    w_in_h = lax.dynamic_slice_in_dim(w_in, y_lo * HID, HID, 1)
    w_out_h = lax.dynamic_slice_in_dim(w_out, y_lo * HID, HID, 0)

    floats = inputs.astype(f32)
    inv_rms = lax.rsqrt(jnp.mean(floats * floats, axis=-1, keepdims=True) + 1e-06)
    normed = floats * inv_rms
    xn_own = (normed * gain_f[None, :]).astype(bf16)
    id_row = jnp.pad(segment_ids.astype(bf16), ((0, 7), (0, D - OWN)))
    packed = jnp.concatenate([xn_own, cotangent, id_row], axis=0)

    row = jnp.stack(gather_step(packed, first_axis))
    plane = jnp.stack(gather_step(row, second_axis))
    other = send(plane, other_core)
    both = jnp.stack([plane, other])
    xn = both[:, :, :, :OWN].reshape(2 * TOK_GROUP, D)
    cot = both[:, :, :, OWN : 2 * OWN].reshape(2 * TOK_GROUP, D)
    ids = both[:, :, :, 2 * OWN, :OWN].astype(f32)

    odd = jnp.array([0.0, 1.0, 1.0, 0.0], f32)
    odd_second = jnp.broadcast_to(odd[:, None], (4, 4))
    odd_first = jnp.broadcast_to(odd[None, :], (4, 4))
    odd_pair = jnp.where(
        core == 0, jnp.stack([odd_second, odd_first]), jnp.stack([odd_first, odd_second])
    )
    labels = ids + SEGS * odd_pair[..., None]
    weights = weights_of(labels.reshape(-1), ids.reshape(-1))
    own_weights = weights[:OWN]

    pre_act = jnp.dot(xn, w_in_h, preferred_element_type=f32)
    act_value, act_slope = gelu_parts(pre_act)
    hidden = (act_value * weights[:, None]).astype(bf16)
    grad_scale = 1.0 / math.sqrt(TOK_GROUP * 16)
    out_grad = (
        lax.dot_general(cot, hidden, (((0,), (0,)), ((), ())), preferred_element_type=f32)
        * grad_scale
    ).astype(bf16)
    hidden_grad = lax.dot_general(
        cot, w_out_h, (((1,), (1,)), ((), ())), preferred_element_type=f32
    )
    pre_grad = (hidden_grad * weights[:, None] * act_slope).astype(bf16)
    in_grad = (
        lax.dot_general(xn, pre_grad, (((0,), (0,)), ((), ())), preferred_element_type=f32)
        * grad_scale
    ).astype(bf16)
    raw = lax.dot_general(
        pre_grad, w_in_h, (((1,), (1,)), ((), ())), preferred_element_type=f32
    )

    out_sum = reduce_z(out_grad, z, 4, 3)
    in_sum = reduce_z(in_grad, z, 3, 4)

    gain_part = jnp.sum(raw * xn.astype(f32), axis=0)
    raw = raw.astype(bf16).reshape(2, 4 * 4 * OWN, D)

    def gain_rows(part):
        high = part.astype(bf16)
        low = (part - high.astype(f32)).astype(bf16)
        return jnp.pad(jnp.stack([high, low]), ((0, 6), (0, 0)))

    def gain_read(rows):
        return rows[0].astype(f32) + rows[1].astype(f32)

    rows = gain_rows(gain_part)
    got = send(jnp.concatenate([raw[1], rows]), other_core)
    raw_own = (raw[0].astype(f32) + got[: TOK_GROUP].astype(f32)).astype(bf16)
    gain_part = gain_part + gain_read(got[TOK_GROUP:])
    for axis, count in ((second_axis, 4 * OWN), (first_axis, OWN)):
        blocks = raw_own.reshape(4, count, D)
        rows = gain_rows(gain_part)
        total = blocks[0].astype(f32)
        gain_part = gain_read(rows)
        for j, o in enumerate(OFFSETS[1:], 1):
            got = send(jnp.concatenate([blocks[j], rows]), axis(o))
            total = total + got[:count].astype(f32)
            gain_part = gain_part + gain_read(got[count:])
        raw_own = total.astype(bf16)
    normed_raw = total
    gain_part = gain_part.reshape(8, 128)
    for o in (1, 2, 4):
        gain_part = gain_part + send(gain_part, xor_z(o))
    gain_grad = gain_part.reshape(D) / gain_f

    ge_own = (cotangent.astype(f32) * own_weights[:, None]).astype(bf16)
    normed_grad = normed_raw * gain_f[None, :]
    inner_mean = jnp.mean(normed_grad * normed, axis=-1, keepdims=True)
    input_grad = (
        ge_own.astype(f32) + inv_rms * (normed_grad - normed * inner_mean)
    ).astype(bf16)

    w_out_grad = join_halves(out_sum, y_lo).T
    w_in_grad = join_halves(in_sum, y_lo)
    return (input_grad, w_in_grad, w_out_grad, gain_grad)


def solution(mesh):
    in_specs = (
        P(("dp", "mp"), None),
        P(("dp", "mp"), None),
        P("dp", "mp"),
        P(),
        P(None, "mp"),
        P("mp", None),
    )
    out_specs = (P(("dp", "mp"), None), P("dp", "mp"), P("mp", "dp"), P())
    return jax.shard_map(body, mesh=mesh, in_specs=in_specs, out_specs=out_specs, check_vma=False)
```

```python
import math

import jax
import jax.numpy as jnp
from jax import lax
from jax.experimental import pallas as pl
from jax.experimental.pallas import tpu as pltpu
from jax.sharding import PartitionSpec as P

TOK_GROUP = 640
SEGS = 8
OWN = 40
ROW = 4 * OWN
CHUNK = 2 * ROW
PLANE = 4 * CHUNK
D = 1024
HID = 1024
PACK = 2 * D + 128
AXES = ("dp", "mp")
OFFSETS = (0, 1, -1, 2)
MIB = 1024 * 1024

GELU_C = 0.7978845608
GELU_A = 0.044715
F32, BF16 = jnp.float32, jnp.bfloat16


def coords(index):
    dp, mp = divmod(index, 16)
    return ((mp // 2) % 4, (mp // 8) * 2 + dp // 8, dp % 8, mp % 2)


def index_of(x, y, z, c):
    x, y, z = x % 4, y % 4, z % 8
    return ((y % 2) * 8 + z) * 16 + ((y // 2) * 4 + x) * 2 + c


def send(value, move):
    pairs = [(i, index_of(*move(*coords(i)))) for i in range(256)]
    return lax.ppermute(value, AXES, pairs)


def first_axis(o):
    return lambda x, y, z, c: (x + o, y, z, c) if c == 0 else (x, y + o, z, c)


def second_axis(o):
    return lambda x, y, z, c: (x, y + o, z, c) if c == 0 else (x + o, y, z, c)


def other_core(x, y, z, c):
    return (x, y, z, 1 - c)


def partner_y(x, y, z, c):
    return (x, y ^ 1, z, c)


def xor_z(o):
    return lambda x, y, z, c: (x, y, z ^ o, c)


def params(mib):
    return pltpu.CompilerParams(vmem_limit_bytes=mib * MIB)


def cost(flops, moved, trans=0):
    return pl.CostEstimate(flops=flops, bytes_accessed=moved, transcendentals=trans)


def pack_kernel(x_ref, cot_ref, label_ref, gain_ref, out_ref):
    floats = x_ref[...].astype(F32)
    inv_rms = lax.rsqrt(jnp.mean(floats * floats, axis=-1, keepdims=True) + 1e-06)
    normed = floats * inv_rms
    out_ref[:, :D] = (normed * gain_ref[...].astype(F32)).astype(BF16)
    out_ref[:, D : 2 * D] = cot_ref[...]
    out_ref[:, 2 * D :] = label_ref[...]


def pack(inputs, cotangent, labels, gain):
    return pl.pallas_call(
        pack_kernel,
        out_shape=jax.ShapeDtypeStruct((OWN, PACK), BF16),
        compiler_params=params(24),
        cost_estimate=cost(OWN * D * 8, 4 * OWN * D * 2),
        name="pack_rows",
    )(inputs, cotangent, labels, gain)


STEPS = 4
WIDTH = HID // STEPS


def chunk_kernel(y_ref, a_ref, b_ref, w_in_ref, w_out_ref, *refs):
    xn_ref, cot_ref, lab_ref, hid_ref, pg_ref, mine_ref, theirs_ref, done_ref, acc = refs[-9:]
    step = pl.program_id(0)

    @pl.when(step == 0)
    def _():
        for k, src in enumerate((a_ref, b_ref)):
            rows = slice(k * ROW, (k + 1) * ROW)
            xn_ref[rows, :] = src[:, :D]
            cot_ref[rows, :] = src[:, D : 2 * D]
            lab_ref[rows, :] = src[:, 2 * D :]
        acc[...] = jnp.zeros_like(acc)

    p = jnp.dot(xn_ref[...], w_in_ref[...], preferred_element_type=F32)
    g = lax.dot_general(
        cot_ref[...], w_out_ref[...], (((1,), (1,)), ((), ())), preferred_element_type=F32
    )
    p2 = p * p
    h = 0.5 * jnp.tanh(p * (GELU_C + (GELU_C * GELU_A) * p2)) + 0.5
    q = p * (2.0 * GELU_C + (6.0 * GELU_C * GELU_A) * p2)
    hid_ref[...] = (p * h).astype(BF16)
    pre_grad = (g * (h * (1.0 + (q - q * h)))).astype(BF16)
    pg_ref[...] = pre_grad
    acc[...] += lax.dot_general(
        pre_grad, w_in_ref[...], (((1,), (1,)), ((), ())), preferred_element_type=F32
    )

    @pl.when(step == STEPS - 1)
    def _():
        mine_ref[...] = acc[:ROW, :].astype(BF16)
        theirs_ref[...] = acc[ROW:, :].astype(BF16)
        done_ref[...] = acc[:8, :128]


def chunk(j, y_lo, a, b, w_in, w_out, full):
    anywhere = pl.BlockSpec(memory_space=pl.ANY)
    fixed = lambda shape: pl.BlockSpec(shape, lambda i, y: (0, 0))
    at_j = lambda shape: pl.BlockSpec(shape, lambda i, y: (j, 0))
    out_specs = [
        at_j((CHUNK, D)),
        at_j((CHUNK, D)),
        at_j((CHUNK, 128)),
        pl.BlockSpec((CHUNK, WIDTH), lambda i, y: (j, i)),
        pl.BlockSpec((CHUNK, WIDTH), lambda i, y: (j, i)),
        at_j((ROW, D)),
        at_j((ROW, D)),
        fixed((8, 128)),
    ]
    shapes = [
        (PLANE, D),
        (PLANE, D),
        (PLANE, 128),
        (PLANE, HID),
        (PLANE, HID),
        (TOK_GROUP, D),
        (TOK_GROUP, D),
    ]
    olds = list(full) if full is not None else []
    return pl.pallas_call(
        chunk_kernel,
        grid_spec=pltpu.PrefetchScalarGridSpec(
            num_scalar_prefetch=1,
            grid=(STEPS,),
            in_specs=[
                fixed((ROW, PACK)),
                fixed((ROW, PACK)),
                pl.BlockSpec((D, WIDTH), lambda i, y: (0, y[0] * STEPS + i)),
                pl.BlockSpec((WIDTH, D), lambda i, y: (y[0] * STEPS + i, 0)),
            ]
            + [anywhere] * len(olds),
            out_specs=out_specs,
            scratch_shapes=[pltpu.VMEM((CHUNK, D), F32)],
        ),
        out_shape=[jax.ShapeDtypeStruct(s, BF16) for s in shapes]
        + [jax.ShapeDtypeStruct((8, 128), F32)],
        input_output_aliases={5 + k: k for k in range(len(olds))},
        compiler_params=params(24),
        cost_estimate=cost(6 * CHUNK * D * HID, 9 * MIB, CHUNK * HID),
        name="chunk_%d" % j,
    )(y_lo, a, b, w_in, w_out, *olds)


def token_weights(labels):
    labels = labels.astype(F32)
    lanes = lax.broadcasted_iota(jnp.int32, (PLANE, 128), 1).astype(F32)
    onehot = jnp.where(labels == lanes, 1.0, 0.0)
    counts = jnp.sum(onehot, axis=0, keepdims=True)
    token_count = jnp.sum(onehot * counts, axis=1, keepdims=True)
    weights = jnp.sqrt(TOK_GROUP / (SEGS * token_count))
    padding = jnp.sum(onehot * jnp.where((lanes == 7.0) | (lanes == 15.0), 1.0, 0.0), axis=1, keepdims=True)
    return jnp.where(padding > 0.5, 0.0, weights)


GRAD_SCALE = 1.0 / math.sqrt(TOK_GROUP * 16)
COLS = 256


def store_grad(out_ref, left_ref, scaled):
    product = lax.dot_general(
        left_ref[...], scaled[...], (((0,), (0,)), ((), ())), preferred_element_type=F32
    )
    out_ref[...] = (product * GRAD_SCALE).astype(BF16).reshape(out_ref.shape)


def out_grad_kernel(lab_ref, cot_ref, hid_ref, out_ref, w_ref, scaled):
    @pl.when(pl.program_id(0) == 0)
    def _():
        weights = token_weights(lab_ref[...])
        scaled[...] = (hid_ref[...].astype(F32) * weights).astype(BF16)
        w_ref[...] = jnp.broadcast_to(weights, (PLANE, 128))

    store_grad(out_ref, cot_ref, scaled)


def in_grad_kernel(
    w_ref, xn_ref, pg_ref, mine_ref, theirs_ref, old_ref, out_ref, gain_ref, scaled
):
    @pl.when(pl.program_id(0) == 0)
    def _():
        scaled[...] = (pg_ref[...].astype(F32) * w_ref[:, :1]).astype(BF16)

    store_grad(out_ref, xn_ref, scaled)
    total = jnp.zeros((1, COLS), F32)
    for j in range(4):
        for k, raw in enumerate((mine_ref, theirs_ref)):
            rows = slice(j * CHUNK + k * ROW, j * CHUNK + (k + 1) * ROW)
            w = jnp.concatenate([w_ref[rows, :]] * (COLS // 128), axis=1)
            term = xn_ref[rows, :].astype(F32) * raw[j * ROW : (j + 1) * ROW, :].astype(F32) * w
            total = total + jnp.sum(term, axis=0, keepdims=True)
    gain_ref[...] = jnp.broadcast_to(total, (8, COLS))


def whole(shape):
    return pl.BlockSpec(shape, lambda i: (0, 0))


def column(rows):
    return pl.BlockSpec((rows, COLS), lambda i: (0, i))


def grad_call(kernel, which, in_specs, args, extra_spec, extra_shape, aliases, name):
    return pl.pallas_call(
        kernel,
        grid=(D // COLS,),
        in_specs=in_specs,
        out_specs=[
            pl.BlockSpec((4, 1, 1, 64, HID), lambda i: (i % 2, which, i // 2, 0, 0)),
            extra_spec,
        ],
        out_shape=[jax.ShapeDtypeStruct((8, 2, 2, 64, HID), BF16), extra_shape],
        scratch_shapes=[pltpu.VMEM((PLANE, HID), BF16)],
        input_output_aliases=aliases,
        compiler_params=params(24),
        cost_estimate=cost(2 * PLANE * D * HID, 8 * MIB),
        name=name,
    )(*args)


def join_halves(summed, y_lo):
    mine = lax.dynamic_index_in_dim(summed, y_lo, 1, False)
    give = lax.dynamic_index_in_dim(summed, 1 - y_lo, 1, False)
    got = send(give, partner_y)
    low = jnp.where(y_lo == 0, mine, got)
    high = jnp.where(y_lo == 0, got, mine)
    return jnp.concatenate([low, high], axis=2)


def gain_rows(part):
    high = part.astype(BF16)
    low = (part - high.astype(F32)).astype(BF16)
    return jnp.pad(jnp.stack([high, low]), ((0, 6), (0, 0)))


def gain_read(rows):
    return rows[0].astype(F32) + rows[1].astype(F32)


def body(inputs, cotangent, segment_ids, norm_gain, w_in, w_out):
    dp = lax.axis_index("dp")
    y_lo, z = lax.div(dp, 8), lax.rem(dp, 8)
    y_arr = y_lo.reshape(1)
    gain_f = norm_gain.astype(F32)

    labels = (segment_ids + SEGS * y_lo).astype(BF16).reshape(OWN, 1)
    labels = jnp.broadcast_to(labels, (OWN, 128))
    packed = pack(inputs, cotangent, labels, norm_gain.reshape(1, D))

    row = jnp.concatenate([packed] + [send(packed, first_axis(-o)) for o in OFFSETS[1:]], axis=0)
    rows = [row] + [send(row, second_axis(-o)) for o in OFFSETS[1:]]
    full = None
    swapped = {0: send(row, other_core)}
    for j in range(4):
        *full, done = chunk(j, y_arr, rows[j], swapped[j], w_in, w_out, full)
        if j < 2:
            for k in ((1, 2), (3,))[j]:
                rows[k] = lax.optimization_barrier((rows[k], done))[0]
                swapped[k] = send(rows[k], other_core)
    xn, cot, lab, hid, pre_grad, mine, theirs = full

    weight_shape = (PLANE, 128)
    grads, weights = grad_call(
        out_grad_kernel,
        0,
        [whole(weight_shape), column(PLANE), whole((PLANE, HID))],
        (lab, cot, hid),
        whole(weight_shape),
        jax.ShapeDtypeStruct(weight_shape, F32),
        {},
        "out_grad",
    )
    grads, gain_part = grad_call(
        in_grad_kernel,
        1,
        [whole(weight_shape), column(PLANE), whole((PLANE, HID))]
        + [column(TOK_GROUP)] * 2
        + [pl.BlockSpec(memory_space=pl.ANY)],
        (weights, xn, pre_grad, mine, theirs, grads),
        column(8),
        jax.ShapeDtypeStruct((8, D), F32),
        {5: 0},
        "in_grad",
    )
    planes = [list(range(8)), list(range(8, 16))]
    summed = lax.psum_scatter(
        grads.reshape(2 * D, HID), "dp", scatter_dimension=0, axis_index_groups=planes, tiled=True
    ).reshape(2, 2, 64, HID)

    total = mine.astype(F32) + send(theirs, other_core).astype(F32)
    gain_part = gain_part + send(gain_part, other_core)
    gain_part = gain_part[0]
    for axis, count in ((second_axis, ROW), (first_axis, OWN)):
        blocks = total.astype(BF16).reshape(4, count, D)
        ride = gain_rows(gain_part)
        total = blocks[0].astype(F32)
        gain_part = gain_read(ride)
        for j, o in enumerate(OFFSETS[1:], 1):
            got = send(jnp.concatenate([blocks[j], ride]), axis(o))
            total = total + got[:count].astype(F32)
            gain_part = gain_part + gain_read(got[count:])
    gain_part = gain_part.reshape(8, 128)
    for o in (1, 2, 4):
        gain_part = gain_part + send(gain_part, xor_z(o))
    gain_grad = gain_part.reshape(D) / gain_f

    floats = inputs.astype(F32)
    inv_rms = lax.rsqrt(jnp.mean(floats * floats, axis=-1, keepdims=True) + 1e-06)
    normed = floats * inv_rms
    own_weights = weights[:OWN, :1]
    normed_raw = total * own_weights
    ge_own = (cotangent.astype(F32) * own_weights).astype(BF16)
    normed_grad = normed_raw * gain_f[None, :]
    inner_mean = jnp.mean(normed_grad * normed, axis=-1, keepdims=True)
    input_grad = (
        ge_own.astype(F32) + inv_rms * (normed_grad - normed * inner_mean)
    ).astype(BF16)

    w_out_grad, w_in_grad = join_halves(summed, y_lo)
    w_out_grad = w_out_grad.T
    return (input_grad, w_in_grad, w_out_grad, gain_grad)


def solution(mesh):
    in_specs = (
        P(("dp", "mp"), None),
        P(("dp", "mp"), None),
        P("dp", "mp"),
        P(),
        P(None, "mp"),
        P("mp", None),
    )
    out_specs = (P(("dp", "mp"), None), P("dp", "mp"), P("mp", "dp"), P())
    return jax.shard_map(body, mesh=mesh, in_specs=in_specs, out_specs=out_specs, check_vma=False)
```

```python
import math

import jax
import jax.numpy as jnp
from jax import lax
from jax.experimental import pallas as pl
from jax.experimental.pallas import tpu as pltpu
from jax.sharding import PartitionSpec as P

TOK_GROUP = 640
SEGS = 8
OWN = 40
ROW = 4 * OWN
CHUNK = 2 * ROW
PLANE = 4 * CHUNK
D = 1024
HID = 1024
PACK = 2 * D + 128
AXES = ("dp", "mp")
OFFSETS = (0, 1, -1, 2)
MIB = 1024 * 1024

GELU_C = 0.7978845608
GELU_A = 0.044715
F32, BF16 = jnp.float32, jnp.bfloat16


def coords(index):
    dp, mp = divmod(index, 16)
    return ((mp // 2) % 4, (mp // 8) * 2 + dp // 8, dp % 8, mp % 2)


def index_of(x, y, z, c):
    x, y, z = x % 4, y % 4, z % 8
    return ((y % 2) * 8 + z) * 16 + ((y // 2) * 4 + x) * 2 + c


def send(value, move):
    pairs = [(i, index_of(*move(*coords(i)))) for i in range(256)]
    return lax.ppermute(value, AXES, pairs)


def first_axis(o):
    return lambda x, y, z, c: (x + o, y, z, c) if c == 0 else (x, y + o, z, c)


def second_axis(o):
    return lambda x, y, z, c: (x, y + o, z, c) if c == 0 else (x + o, y, z, c)


def other_core(x, y, z, c):
    return (x, y, z, 1 - c)


def partner_y(x, y, z, c):
    return (x, y ^ 1, z, c)


def xor_z(o):
    return lambda x, y, z, c: (x, y, z ^ o, c)


def params(mib):
    return pltpu.CompilerParams(vmem_limit_bytes=mib * MIB)


def cost(flops, moved, trans=0):
    return pl.CostEstimate(flops=flops, bytes_accessed=moved, transcendentals=trans)


def pack_kernel(y_ref, x_ref, cot_ref, ids_ref, gain_ref, out_ref):
    floats = x_ref[...].astype(F32)
    inv_rms = lax.rsqrt(jnp.mean(floats * floats, axis=-1, keepdims=True) + 1e-06)
    normed = floats * inv_rms
    out_ref[:, :D] = cot_ref[...]
    out_ref[:, D : 2 * D] = (normed * gain_ref[...].astype(F32).reshape(1, D)).astype(BF16)
    ids = jnp.broadcast_to((ids_ref[...] + SEGS * y_ref[0]).astype(F32), (OWN, OWN))
    along = lax.broadcasted_iota(jnp.int32, (OWN, OWN), 0)
    across = lax.broadcasted_iota(jnp.int32, (OWN, OWN), 1)
    label = jnp.sum(jnp.where(along == across, ids, 0.0), axis=1, keepdims=True)
    out_ref[:, 2 * D :] = jnp.broadcast_to(label, (OWN, 128)).astype(BF16)


def pack(y_lo, inputs, cotangent, ids, gain):
    return pl.pallas_call(
        pack_kernel,
        in_specs=[pl.BlockSpec(memory_space=pltpu.SMEM)]
        + [pl.BlockSpec(memory_space=pltpu.VMEM)] * 4,
        out_shape=jax.ShapeDtypeStruct((OWN, PACK), BF16),
        compiler_params=params(4),
        cost_estimate=cost(OWN * D * 8, 4 * OWN * D * 2),
        name="pack_rows",
    )(y_lo, inputs, cotangent, ids, gain)


def nothing(*refs):
    pass


def after(values, *first):
    anywhere = pl.BlockSpec(memory_space=pl.ANY)
    return pl.pallas_call(
        nothing,
        in_specs=[anywhere] * (len(values) + len(first)),
        out_specs=[anywhere] * len(values),
        out_shape=[jax.ShapeDtypeStruct(v.shape, v.dtype) for v in values],
        input_output_aliases={k: k for k in range(len(values))},
        compiler_params=params(1),
        cost_estimate=cost(0, 0),
        name="after",
    )(*values, *first)


STEPS = 4
WIDTH = HID // STEPS


def chunk_kernel(a_ref, b_ref, w_in_ref, w_out_ref, left_ref, lab_ref, right_ref, mine_ref, theirs_ref, acc):
    for k, src in enumerate((a_ref, b_ref)):
        rows = slice(k * ROW, (k + 1) * ROW)
        left_ref[rows, :] = src[:, : 2 * D]
        lab_ref[rows, :] = src[:, 2 * D :]
    for step in range(STEPS):
        cols = slice(step * WIDTH, (step + 1) * WIDTH)
        p = jnp.dot(left_ref[:, D:], w_in_ref[:, cols], preferred_element_type=F32)
        g = lax.dot_general(
            left_ref[:, :D], w_out_ref[cols, :], (((1,), (1,)), ((), ())), preferred_element_type=F32
        )
        p2 = p * p
        h = 0.5 * jnp.tanh(p * (GELU_C + (GELU_C * GELU_A) * p2)) + 0.5
        q = p * (2.0 * GELU_C + (6.0 * GELU_C * GELU_A) * p2)
        right_ref[:, cols] = (p * h).astype(BF16)
        pre_grad = (g * (h * (1.0 + (q - q * h)))).astype(BF16)
        right_ref[:, HID + step * WIDTH : HID + (step + 1) * WIDTH] = pre_grad
        raw = lax.dot_general(
            pre_grad, w_in_ref[:, cols], (((1,), (1,)), ((), ())), preferred_element_type=F32
        )
        if step == 0:
            acc[...] = raw
        elif step < STEPS - 1:
            acc[...] += raw
        else:
            mine_ref[...] = (acc[:ROW, :] + raw[:ROW]).astype(BF16)
            theirs_ref[...] = (acc[ROW:, :] + raw[ROW:]).astype(BF16)


def chunk(j, a, b, w_in, w_out):
    here = pl.BlockSpec(memory_space=pltpu.VMEM)
    shapes = [(CHUNK, 2 * D), (CHUNK, 128), (CHUNK, 2 * HID), (ROW, D), (ROW, D)]
    return pl.pallas_call(
        chunk_kernel,
        in_specs=[here] * 4,
        out_specs=[here] * 5,
        scratch_shapes=[pltpu.VMEM((CHUNK, D), F32)],
        out_shape=[jax.ShapeDtypeStruct(s, BF16) for s in shapes],
        compiler_params=params(16),
        cost_estimate=cost(6 * CHUNK * D * HID, 9 * MIB, CHUNK * HID),
        name="chunk_%d" % j,
    )(a, b, w_in, w_out)


def token_weights(labels):
    labels = labels.astype(F32)
    lanes = lax.broadcasted_iota(jnp.int32, (PLANE, 128), 1).astype(F32)
    onehot = jnp.where(labels == lanes, 1.0, 0.0)
    counts = jnp.sum(onehot, axis=0, keepdims=True)
    token_count = jnp.sum(onehot * counts, axis=1, keepdims=True)
    weights = jnp.sqrt(TOK_GROUP / (SEGS * token_count))
    padding = jnp.sum(onehot * jnp.where((lanes == 7.0) | (lanes == 15.0), 1.0, 0.0), axis=1, keepdims=True)
    return jnp.where(padding > 0.5, 0.0, weights)


GRAD_SCALE = 1.0 / math.sqrt(TOK_GROUP * 16)
COLS = 256


BLOCKS = D // COLS


def grads_kernel(*refs):
    labs, lefts, rights, raws = refs[:4], refs[4:8], refs[8:12], refs[12:20]
    out_ref, gain_ref, own_ref, weight = refs[20:]
    step = pl.program_id(0)

    @pl.when(step == 0)
    def _():
        weights = token_weights(jnp.concatenate([lab[...] for lab in labs], axis=0))
        weight[...] = jnp.broadcast_to(weights, (PLANE, 128))
        own_ref[...] = jnp.broadcast_to(weights[:OWN], (OWN, 128))

    def product(array, block):
        cols = pl.ds(pl.multiple_of(step * COLS, COLS), COLS)
        left = jnp.concatenate([ref[:, cols] for ref in lefts], axis=0).astype(F32)
        left = left * jnp.concatenate([weight[...]] * (COLS // 128), axis=1)
        right = jnp.concatenate([ref[:, array * HID : (array + 1) * HID] for ref in rights], axis=0)
        total = lax.dot_general(
            left.astype(BF16), right, (((0,), (0,)), ((), ())), preferred_element_type=F32
        )
        out_ref[...] = (total * GRAD_SCALE).astype(BF16).reshape(out_ref.shape)
        return left

    @pl.when(step < BLOCKS)
    def _():
        product(0, step)

    @pl.when(step >= BLOCKS)
    def _():
        left = product(1, step)
        cols = pl.ds(pl.multiple_of((step - BLOCKS) * COLS, COLS), COLS)
        raw = jnp.concatenate([ref[:, cols] for ref in raws], axis=0).astype(F32)
        total = jnp.sum(left * raw, axis=0, keepdims=True)
        gain_ref[...] = jnp.broadcast_to(total, (8, COLS))


def grads_call(labs, lefts, rights, raws):
    here = pl.BlockSpec(memory_space=pltpu.VMEM)
    place = lambda i: (i % 2, i // BLOCKS, (i % BLOCKS) // 2, 0, 0)
    return pl.pallas_call(
        grads_kernel,
        grid=(2 * BLOCKS,),
        in_specs=[here] * 20,
        out_specs=[
            pl.BlockSpec((4, 1, 1, 64, HID), place),
            pl.BlockSpec((8, COLS), lambda i: (0, jnp.maximum(i - BLOCKS, 0))),
            pl.BlockSpec((OWN, 128), lambda i: (0, 0)),
        ],
        out_shape=[
            pltpu.HBM((8, 2, 2, 64, HID), BF16),
            jax.ShapeDtypeStruct((8, D), F32),
            jax.ShapeDtypeStruct((OWN, 128), F32),
        ],
        scratch_shapes=[pltpu.VMEM((PLANE, 128), F32)],
        compiler_params=params(16),
        cost_estimate=cost(4 * PLANE * D * HID, 24 * MIB),
        name="weight_grads",
    )(*labs, *lefts, *rights, *raws)


def join_halves(summed, y_lo):
    mine = lax.dynamic_index_in_dim(summed, y_lo, 1, False)
    give = lax.dynamic_index_in_dim(summed, 1 - y_lo, 1, False)
    got = send(give, partner_y)
    low = jnp.where(y_lo == 0, mine, got)
    high = jnp.where(y_lo == 0, got, mine)
    return jnp.concatenate([low, high], axis=2)


def gain_rows(part):
    high = part.astype(BF16)
    low = (part - high.astype(F32)).astype(BF16)
    return jnp.pad(jnp.stack([high, low]), ((0, 6), (0, 0)))


def gain_read(rows):
    return rows[0].astype(F32) + rows[1].astype(F32)


def body(inputs, cotangent, segment_ids, norm_gain, w_in, w_out):
    dp = lax.axis_index("dp")
    y_lo, z = lax.div(dp, 8), lax.rem(dp, 8)
    y_arr = y_lo.reshape(1)
    gain_f = norm_gain.astype(F32)

    packed = pack(y_arr, inputs, cotangent, segment_ids, norm_gain)

    row = jnp.concatenate([packed] + [send(packed, first_axis(-o)) for o in OFFSETS[1:]], axis=0)
    w_in = lax.dynamic_slice_in_dim(w_in, y_lo * HID, HID, 1)
    w_out = lax.dynamic_slice_in_dim(w_out, y_lo * HID, HID, 0)
    (row,) = after([row], w_in, w_out)
    half = ROW // 2
    rows = [row, send(row, second_axis(-1)), send(row, second_axis(1))]
    swapped = [send(row, other_core)]
    parts = []
    for j in range(4):
        parts.append(chunk(j, rows[j], swapped[j], w_in, w_out))
        done = parts[j][1]
        if j == 0:
            plus, minus = rows[1:] = after(rows[1:], done)
            relayed = [send(plus[:half], second_axis(-1)), send(minus[half:], second_axis(1))]
            swapped += [send(plus, other_core), send(minus, other_core)]
        if j == 1:
            relayed = after(relayed, done)
            rows.append(jnp.concatenate(relayed, axis=0))
            swapped.append(send(rows[3], other_core))
    lefts, labs, rights, mine, theirs = zip(*parts)
    raws = [raw for pair in zip(mine, theirs) for raw in pair]
    grads, gain_part, own_weights = grads_call(labs, lefts, rights, raws)
    mine, theirs = jnp.concatenate(mine), jnp.concatenate(theirs)
    planes = [list(range(8)), list(range(8, 16))]
    summed = lax.psum_scatter(
        grads.reshape(2 * D, HID), "dp", scatter_dimension=0, axis_index_groups=planes, tiled=True
    ).reshape(2, 2, 64, HID)

    total = mine.astype(F32) + send(theirs, other_core).astype(F32)
    gain_part = gain_part + send(gain_part, other_core)
    gain_part = gain_part[0]
    for axis, count in ((second_axis, ROW), (first_axis, OWN)):
        blocks = total.astype(BF16).reshape(4, count, D)
        ride = gain_rows(gain_part)
        total = blocks[0].astype(F32)
        gain_part = gain_read(ride)
        for j, o in enumerate(OFFSETS[1:], 1):
            got = send(jnp.concatenate([blocks[j], ride]), axis(o))
            total = total + got[:count].astype(F32)
            gain_part = gain_part + gain_read(got[count:])
    gain_part = gain_part.reshape(8, 128)
    for o in (1, 2, 4):
        gain_part = gain_part + send(gain_part, xor_z(o))
    gain_grad = gain_part.reshape(D) / gain_f

    floats = inputs.astype(F32)
    inv_rms = lax.rsqrt(jnp.mean(floats * floats, axis=-1, keepdims=True) + 1e-06)
    normed = floats * inv_rms
    own_weights = own_weights[:, :1]
    normed_raw = total * own_weights
    ge_own = (cotangent.astype(F32) * own_weights).astype(BF16)
    normed_grad = normed_raw * gain_f[None, :]
    inner_mean = jnp.mean(normed_grad * normed, axis=-1, keepdims=True)
    input_grad = (
        ge_own.astype(F32) + inv_rms * (normed_grad - normed * inner_mean)
    ).astype(BF16)

    w_out_grad, w_in_grad = join_halves(summed, y_lo)
    w_out_grad = w_out_grad.T
    return (input_grad, w_in_grad, w_out_grad, gain_grad)


def solution(mesh):
    in_specs = (
        P(("dp", "mp"), None),
        P(("dp", "mp"), None),
        P("dp", "mp"),
        P(),
        P(None, "mp"),
        P("mp", None),
    )
    out_specs = (P(("dp", "mp"), None), P("dp", "mp"), P("mp", "dp"), P())
    return jax.shard_map(body, mesh=mesh, in_specs=in_specs, out_specs=out_specs, check_vma=False)
```

```python
import functools
import math

import jax
import jax.numpy as jnp
from jax import lax
from jax.experimental import pallas as pl
from jax.experimental.pallas import tpu as pltpu
from jax.sharding import PartitionSpec as P

TOK_GROUP = 640
SEGS = 8
OWN = 40
ROW = 4 * OWN
CHUNK = 2 * ROW
PLANE = 4 * CHUNK
D = 1024
HID = 1024
PACK = 2 * D + 128
AXES = ("dp", "mp")
OFFSETS = (0, 1, -1, 2)
MIB = 1024 * 1024

GELU_C = 0.7978845608
GELU_A = 0.044715
F32, BF16 = jnp.float32, jnp.bfloat16


def coords(index):
    dp, mp = divmod(index, 16)
    return ((mp // 2) % 4, (mp // 8) * 2 + dp // 8, dp % 8, mp % 2)


def index_of(x, y, z, c):
    x, y, z = x % 4, y % 4, z % 8
    return ((y % 2) * 8 + z) * 16 + ((y // 2) * 4 + x) * 2 + c


def send(value, move):
    pairs = [(i, index_of(*move(*coords(i)))) for i in range(256)]
    return lax.ppermute(value, AXES, pairs)


def first_axis(o):
    return lambda x, y, z, c: (x + o, y, z, c) if c == 0 else (x, y + o, z, c)


def second_axis(o):
    return lambda x, y, z, c: (x, y + o, z, c) if c == 0 else (x + o, y, z, c)


def other_core(x, y, z, c):
    return (x, y, z, 1 - c)


def partner_y(x, y, z, c):
    return (x, y ^ 1, z, c)


def along_z(o):
    return lambda x, y, z, c: (x, y, z + o, c)


def xor_z(o):
    return lambda x, y, z, c: (x, y, z ^ o, c)


def params(mib):
    return pltpu.CompilerParams(vmem_limit_bytes=mib * MIB)


def cost(flops, moved, trans=0):
    return pl.CostEstimate(flops=flops, bytes_accessed=moved, transcendentals=trans)


def here(count):
    return [pl.BlockSpec(memory_space=pltpu.VMEM)] * count


def scalar():
    return pl.BlockSpec(memory_space=pltpu.SMEM)


def shape(*dims, dtype=BF16):
    return jax.ShapeDtypeStruct(dims, dtype)


def pack_kernel(spot_ref, x_hbm, cot_hbm, ids_hbm, gain_hbm, out_ref, x_ref, cot_ref, ids_ref, gain_ref, sems):
    copies = [
        pltpu.make_async_copy(src, dst, sems.at[k])
        for k, (src, dst) in enumerate(
            [(x_hbm, x_ref), (cot_hbm, cot_ref), (ids_hbm, ids_ref), (gain_hbm, gain_ref)]
        )
    ]
    for copy in copies:
        copy.start()
    for copy in copies:
        copy.wait()
    floats = x_ref[...].astype(F32)
    inv_rms = lax.rsqrt(jnp.mean(floats * floats, axis=-1, keepdims=True) + 1e-06)
    normed = floats * inv_rms
    out_ref[:, :D] = cot_ref[...]
    out_ref[:, D : 2 * D] = (normed * gain_ref[...].astype(F32).reshape(1, D)).astype(BF16)
    ids = jnp.broadcast_to((ids_ref[...] + SEGS * spot_ref[0]).astype(F32), (OWN, OWN))
    along = lax.broadcasted_iota(jnp.int32, (OWN, OWN), 0)
    across = lax.broadcasted_iota(jnp.int32, (OWN, OWN), 1)
    label = jnp.sum(jnp.where(along == across, ids, 0.0), axis=1, keepdims=True)
    out_ref[:, 2 * D :] = jnp.broadcast_to(label, (OWN, 128)).astype(BF16)


def pack(spot, inputs, cotangent, ids, gain):
    inputs_in_hbm = [
        pltpu.with_memory_space_constraint(a, pltpu.HBM) for a in (inputs, cotangent, ids, gain)
    ]
    return pl.pallas_call(
        pack_kernel,
        in_specs=[pl.BlockSpec(memory_space=pltpu.SMEM)]
        + [pl.BlockSpec(memory_space=pltpu.HBM)] * 4,
        out_shape=jax.ShapeDtypeStruct((OWN, PACK), BF16),
        scratch_shapes=[
            pltpu.VMEM((OWN, D), BF16),
            pltpu.VMEM((OWN, D), BF16),
            pltpu.VMEM((1, OWN), jnp.int32),
            pltpu.VMEM((D,), BF16),
            pltpu.SemaphoreType.DMA((4,)),
        ],
        compiler_params=params(4),
        cost_estimate=cost(OWN * D * 8, 4 * OWN * D * 2),
        name="pack_rows",
    )(spot, *inputs_in_hbm)


def nothing(*refs):
    pass


def after(values, *first):
    anywhere = pl.BlockSpec(memory_space=pl.ANY)
    return pl.pallas_call(
        nothing,
        in_specs=[anywhere] * (len(values) + len(first)),
        out_specs=[anywhere] * len(values),
        out_shape=[jax.ShapeDtypeStruct(v.shape, v.dtype) for v in values],
        input_output_aliases={k: k for k in range(len(values))},
        compiler_params=params(1),
        cost_estimate=cost(0, 0),
        name="after",
    )(*values, *first)


def relay_halves(plus, minus, *first):
    def kernel(plus_ref, minus_ref, *refs):
        refs[-2][...] = plus_ref[: ROW // 2, :]
        refs[-1][...] = minus_ref[ROW // 2 :, :]

    return pl.pallas_call(
        kernel,
        in_specs=here(2) + [pl.BlockSpec(memory_space=pl.ANY)] * len(first),
        out_specs=tuple(here(2)),
        out_shape=(shape(ROW // 2, PACK),) * 2,
        compiler_params=params(2),
        cost_estimate=cost(0, MIB),
        name="relay_halves",
    )(plus, minus, *first)


STEPS = 4
WIDTH = HID // STEPS


def chunk_kernel(count, *refs):
    srcs, (w_in_ref, w_out_ref) = refs[:count], refs[count : count + 2]
    left_ref, lab_ref, right_ref, mine_ref, theirs_ref, acc = refs[count + 2 :]
    size = CHUNK // count
    for k, src in enumerate(srcs):
        rows = slice(k * size, (k + 1) * size)
        left_ref[rows, :] = src[:, : 2 * D]
        lab_ref[rows, :] = src[:, 2 * D :]
    for step in range(STEPS):
        cols = slice(step * WIDTH, (step + 1) * WIDTH)
        p = jnp.dot(left_ref[:, D:], w_in_ref[:, cols], preferred_element_type=F32)
        g = lax.dot_general(
            left_ref[:, :D], w_out_ref[cols, :], (((1,), (1,)), ((), ())), preferred_element_type=F32
        )
        p2 = p * p
        h = 0.5 * jnp.tanh(p * (GELU_C + (GELU_C * GELU_A) * p2)) + 0.5
        q = p * (2.0 * GELU_C + (6.0 * GELU_C * GELU_A) * p2)
        right_ref[:, cols] = (p * h).astype(BF16)
        pre_grad = (g * (h * (1.0 + (q - q * h)))).astype(BF16)
        right_ref[:, HID + step * WIDTH : HID + (step + 1) * WIDTH] = pre_grad
        raw = lax.dot_general(
            pre_grad, w_in_ref[:, cols], (((1,), (1,)), ((), ())), preferred_element_type=F32
        )
        if step == 0:
            acc[...] = raw
        elif step < STEPS - 1:
            acc[...] += raw
        else:
            mine_ref[...] = (acc[:ROW, :] + raw[:ROW]).astype(BF16)
            theirs_ref[...] = (acc[ROW:, :] + raw[ROW:]).astype(BF16)


def chunk(j, srcs, w_in, w_out):
    shapes = [(CHUNK, 2 * D), (CHUNK, 128), (CHUNK, 2 * HID), (ROW, D), (ROW, D)]
    return pl.pallas_call(
        functools.partial(chunk_kernel, len(srcs)),
        in_specs=here(len(srcs) + 2),
        out_specs=here(5),
        scratch_shapes=[pltpu.VMEM((CHUNK, D), F32)],
        out_shape=[shape(*s) for s in shapes],
        compiler_params=params(8),
        cost_estimate=cost(6 * CHUNK * D * HID, 9 * MIB, CHUNK * HID),
        name="chunk_%d" % j,
    )(*srcs, w_in, w_out)


def token_weights(labels):
    labels = labels.astype(F32)
    lanes = lax.broadcasted_iota(jnp.int32, (PLANE, 128), 1).astype(F32)
    onehot = jnp.where(labels == lanes, 1.0, 0.0)
    counts = jnp.sum(onehot, axis=0, keepdims=True)
    token_count = jnp.sum(onehot * counts, axis=1, keepdims=True)
    weights = jnp.sqrt(TOK_GROUP / (SEGS * token_count))
    padding = jnp.sum(onehot * jnp.where((lanes == 7.0) | (lanes == 15.0), 1.0, 0.0), axis=1, keepdims=True)
    return jnp.where(padding > 0.5, 0.0, weights)


GRAD_SCALE = 1.0 / math.sqrt(TOK_GROUP * 16)


RIDE = 16


def gain_call(weight, lefts, raws, *first):
    def kernel(w_ref, *refs):
        lefts, raws, gain_ref = refs[:4], refs[4:12], refs[-1]
        total = jnp.zeros((1, D), F32)
        for k, raw in enumerate(raws):
            rows = slice((k % 2) * ROW, (k % 2 + 1) * ROW)
            w = w_ref[k * ROW : (k + 1) * ROW, :1]
            term = lefts[k // 2][rows, D:].astype(F32) * raw[...].astype(F32) * w
            total = total + jnp.sum(term, axis=0, keepdims=True)
        gain_ref[...] = jnp.broadcast_to(total, (8, D))

    anywhere = pl.BlockSpec(memory_space=pl.ANY)
    return pl.pallas_call(
        kernel,
        in_specs=here(13) + [anywhere] * len(first),
        out_shape=shape(8, D, dtype=F32),
        compiler_params=params(8),
        cost_estimate=cost(4 * PLANE * D, 8 * MIB),
        name="gain_term",
    )(weight, *lefts, *raws, *first)


def term_block(array, offsets, z, weight, lefts, rights):
    lane = lax.broadcasted_iota(jnp.int32, (PLANE, 128), 1)
    blocks = []
    for offset in offsets:
        to = lax.rem(z + offset + 8, 8)
        shift = lax.rem(to, 2) * 64
        halves = []
        for y in range(2):
            start = pl.multiple_of(array * D + y * (D // 2) + (to // 2) * 128, 128)
            left = jnp.concatenate([ref[:, pl.ds(start, 128)] for ref in lefts], axis=0).astype(F32)
            halves.append(pltpu.roll(left * weight, shift if y == 0 else 64 - shift, 1))
        blocks.append(jnp.where(lane < 64, *halves).astype(BF16))
    left = jnp.concatenate(blocks, axis=1)
    right = jnp.concatenate([ref[:, array * HID : (array + 1) * HID] for ref in rights], axis=0)
    total = lax.dot_general(left, right, (((0,), (0,)), ((), ())), preferred_element_type=F32)
    return (total * GRAD_SCALE).astype(BF16)


def far_call(spot, labs, lefts, rights, theirs):
    def kernel(spot_ref, *refs):
        labs, lefts, rights, theirs = refs[:4], refs[4:8], refs[8:12], refs[12:16]
        weight_ref, up_ref, down_ref, theirs_ref = refs[16:]
        weights = token_weights(jnp.concatenate([lab[...] for lab in labs], axis=0))
        weight_ref[...] = jnp.broadcast_to(weights, (PLANE, 128))
        for array, ref in enumerate((up_ref, down_ref)):
            block = term_block(array, (4,), spot_ref[1], weight_ref[...], lefts, rights)
            ref[...] = block.reshape(2, 64, HID)
        for j, raw in enumerate(theirs):
            theirs_ref[j * ROW : (j + 1) * ROW, :] = raw[...]

    return pl.pallas_call(
        kernel,
        in_specs=[scalar()] + here(16),
        out_specs=tuple(here(4)),
        out_shape=(
            shape(PLANE, 128, dtype=F32),
            shape(2, 64, HID),
            shape(2, 64, HID),
            shape(TOK_GROUP, D),
        ),
        compiler_params=params(12),
        cost_estimate=cost(PLANE * D * HID, 8 * MIB),
        name="far_terms",
    )(spot, *labs, *lefts, *rights, *theirs)


def terms_call(name, groups, spot, weight, lefts, rights, *first):
    count = sum(len(group) for group in groups)

    def kernel(spot_ref, weight_ref, *refs):
        lefts, rights, out_ref = refs[:4], refs[4:8], refs[-1]
        at = 0
        for group in groups:
            for array in range(2):
                block = term_block(array, group, spot_ref[1], weight_ref[...], lefts, rights)
                block = block.reshape(len(group), 2, 64, HID)
                for k in range(len(group)):
                    out_ref[at + k, array] = block[k]
            at += len(group)

    return pl.pallas_call(
        kernel,
        in_specs=[scalar()] + here(9) + [pl.BlockSpec(memory_space=pl.ANY)] * len(first),
        out_specs=here(1)[0],
        out_shape=shape(count, 2, 2, 64, HID),
        compiler_params=params(12),
        cost_estimate=cost(count * PLANE * 512 * HID, 8 * MIB),
        name=name,
    )(spot, weight, *lefts, *rights, *first)


def add(*terms):
    return sum(t.astype(F32) for t in terms).astype(BF16)


def ring_call(step, at, terms, plus, minus, *first):
    def kernel(terms_ref, plus_ref, minus_ref, *refs):
        up_ref, down_ref = refs[-2:]
        if step == 1:
            up_ref[0] = add(plus_ref[...], terms_ref[at, 0])
            up_ref[1] = terms_ref[at, 1]
            down_ref[0] = terms_ref[at + 1, 0]
            down_ref[1] = add(minus_ref[...], terms_ref[at + 1, 1])
        else:
            for array in range(2):
                up_ref[array] = add(plus_ref[array], terms_ref[at, array])
                down_ref[array] = add(minus_ref[array], terms_ref[at + 1, array])

    anywhere = pl.BlockSpec(memory_space=pl.ANY)
    return pl.pallas_call(
        kernel,
        in_specs=here(3) + [anywhere] * len(first),
        out_specs=tuple(here(2)),
        out_shape=(shape(2, 2, 64, HID),) * 2,
        compiler_params=params(4),
        cost_estimate=cost(4 * MIB, 4 * MIB),
        name="ring_%d" % step,
    )(terms, plus, minus, *first)


def ring_last(spot, at, terms, plus, minus, *first):
    def kernel(spot_ref, terms_ref, plus_ref, minus_ref, *refs):
        mine_ref, give_ref = refs[-2:]
        own = spot_ref[0]
        for array in range(2):
            for ref, y in ((give_ref, 1 - own), (mine_ref, own)):
                ref[array] = add(terms_ref[at, array, y], plus_ref[array, y], minus_ref[array, y])

    anywhere = pl.BlockSpec(memory_space=pl.ANY)
    return pl.pallas_call(
        kernel,
        in_specs=[scalar()] + here(3) + [anywhere] * len(first),
        out_specs=tuple(here(2)),
        out_shape=(shape(2, 64, HID),) * 2,
        compiler_params=params(4),
        cost_estimate=cost(MIB, 2 * MIB),
        name="ring_last",
    )(spot, terms, plus, minus, *first)


def place(spot, mine, got):
    def kernel(spot_ref, mine_ref, got_ref, *outs):
        for y in range(2):

            @pl.when(spot_ref[0] == y)
            def _():
                for array, out in enumerate(outs):
                    out[:, y * HID : (y + 1) * HID] = mine_ref[array]
                    out[:, (1 - y) * HID : (2 - y) * HID] = got_ref[array]

    return pl.pallas_call(
        kernel,
        in_specs=[scalar()] + here(2),
        out_specs=tuple(here(2)),
        out_shape=(shape(64, 2 * HID),) * 2,
        compiler_params=params(4),
        cost_estimate=cost(64 * MIB, 32 * MIB),
        name="place",
    )(spot, mine, got)


def ride_rows(total):
    high = total.astype(BF16).astype(F32)
    rows = lax.broadcasted_iota(jnp.int32, (RIDE, D), 0)
    return jnp.where(rows == 0, high, jnp.where(rows == 1, total - high, 0.0)).astype(BF16)


def ride_sum(rows):
    return jnp.sum(rows.astype(F32), axis=0, keepdims=True)


def raw_first(mine, got, gain, *first):
    def kernel(*refs):
        mines, got_ref, gain_ref = refs[:4], refs[4], refs[5]
        keep_ref, *sends = refs[-4:]
        keep_ref[...] = mines[0][...].astype(F32) + got_ref[:ROW, :].astype(F32)
        ride = ride_rows(gain_ref[:1, :])
        for j in range(1, 4):
            sends[j - 1][:ROW, :] = add(mines[j][...], got_ref[j * ROW : (j + 1) * ROW, :])
            sends[j - 1][ROW:, :] = ride

    anywhere = pl.BlockSpec(memory_space=pl.ANY)
    return pl.pallas_call(
        kernel,
        in_specs=here(6) + [anywhere] * len(first),
        out_specs=tuple(here(4)),
        out_shape=(shape(ROW, D, dtype=F32),) + (shape(ROW + RIDE, D),) * 3,
        compiler_params=params(4),
        cost_estimate=cost(2 * MIB, 4 * MIB),
        name="raw_first",
    )(*mine, got, gain, *first)


def raw_second(keep, gain, gots, *first):
    def kernel(keep_ref, gain_ref, *refs):
        gots = refs[:3]
        mine_ref, total_ref, *sends = refs[-5:]
        total = keep_ref[...]
        row = ride_sum(ride_rows(gain_ref[:1, :]))
        for got in gots:
            total = total + got[:ROW, :].astype(F32)
            row = row + ride_sum(got[ROW:, :])
        ride = ride_rows(row)
        mine_ref[...] = total[:OWN]
        total_ref[...] = jnp.broadcast_to(ride_sum(ride), (8, D))
        for j in range(1, 4):
            block = jnp.concatenate([total[j * OWN : (j + 1) * OWN], jnp.zeros((8, D), F32)], axis=0)
            sends[j - 1][: OWN + 8, :] = block.astype(BF16)
            sends[j - 1][OWN + 8 :, :] = ride

    anywhere = pl.BlockSpec(memory_space=pl.ANY)
    return pl.pallas_call(
        kernel,
        in_specs=here(5) + [anywhere] * len(first),
        out_specs=tuple(here(5)),
        out_shape=(shape(OWN, D, dtype=F32), shape(8, D, dtype=F32))
        + (shape(OWN + 8 + RIDE, D),) * 3,
        compiler_params=params(6),
        cost_estimate=cost(2 * MIB, 2 * MIB),
        name="raw_second",
    )(keep, gain, *gots, *first)


def raw_last(mine, row, gots, weight, inputs, cotangent, gain, *first):
    def kernel(mine_ref, row_ref, *refs):
        gots, (w_ref, x_ref, cot_ref, gain_ref), (grad_ref, gain_out) = refs[:3], refs[3:7], refs[-2:]
        raw, row = mine_ref[...], row_ref[:1, :]
        for got in gots:
            raw = raw + got[: OWN + 8, :].astype(F32)[:OWN]
            row = row + ride_sum(got[OWN + 8 :, :])
        gain = gain_ref[...].astype(F32).reshape(1, D)
        gain_out[...] = jnp.broadcast_to(row / gain, (8, D))
        w = w_ref[:OWN, :1]
        floats = x_ref[...].astype(F32)
        inv_rms = lax.rsqrt(jnp.mean(floats * floats, axis=-1, keepdims=True) + 1e-06)
        normed = floats * inv_rms
        dn = raw * w * gain
        inner = jnp.mean(dn * normed, axis=-1, keepdims=True)
        ge = (cot_ref[...].astype(F32) * w).astype(BF16).astype(F32)
        grad_ref[...] = (ge + inv_rms * (dn - normed * inner)).astype(BF16)

    return pl.pallas_call(
        kernel,
        in_specs=here(9) + [pl.BlockSpec(memory_space=pl.ANY)] * len(first),
        out_specs=tuple(here(2)),
        out_shape=(shape(OWN, D), shape(8, D, dtype=F32)),
        compiler_params=params(4),
        cost_estimate=cost(MIB, MIB),
        name="raw_last",
    )(mine, row, *gots, weight, inputs, cotangent, gain, *first)


def body(inputs, cotangent, segment_ids, norm_gain, w_in, w_out):
    dp = lax.axis_index("dp")
    y_lo, z = lax.div(dp, 8), lax.rem(dp, 8)
    spot = jnp.stack([y_lo, z])
    packed = pack(spot, inputs, cotangent, segment_ids, norm_gain)

    row = jnp.concatenate([packed] + [send(packed, first_axis(-o)) for o in OFFSETS[1:]], axis=0)
    w_in = lax.dynamic_slice_in_dim(w_in, y_lo * HID, HID, 1)
    w_out = lax.dynamic_slice_in_dim(w_out, y_lo * HID, HID, 0)
    (row,) = after([row], w_in, w_out)
    plus, minus = send(row, second_axis(-1)), send(row, second_axis(1))
    parts = [chunk(0, [row, send(row, other_core)], w_in, w_out)]
    plus, minus = after([plus, minus], parts[0][1])
    relayed = [
        send(part, second_axis(o)) for part, o in zip(relay_halves(plus, minus), (-1, 1))
    ]
    parts.append(chunk(1, [plus, send(plus, other_core)], w_in, w_out))
    relayed = after(relayed, parts[1][1])
    parts.append(chunk(2, [minus, send(minus, other_core)], w_in, w_out))
    parts.append(chunk(3, [*relayed, *(send(r, other_core) for r in relayed)], w_in, w_out))
    lefts, labs, rights, mine, theirs = zip(*parts)

    weight, up, down, theirs_all = far_call(spot, labs, lefts, rights, theirs)
    up_got, down_got = send(up, along_z(1)), send(down, along_z(-1))
    raw_got = send(theirs_all, other_core)
    near = terms_call("near_terms", [(3, -3)], spot, weight, lefts, rights)
    raws = [raw for pair in zip(mine, theirs) for raw in pair]
    gain = gain_call(weight, lefts, raws, near)
    keep, *blocks = raw_first(mine, raw_got, gain)
    gots = [send(b, second_axis(o)) for b, o in zip(blocks, OFFSETS[1:])]

    up, down = ring_call(1, 0, near, up_got, down_got, *blocks)
    up_got, down_got = send(up, along_z(1)), send(down, along_z(-1))
    rest = terms_call("rest_terms", [(2, -2), (1, -1), (0,)], spot, weight, lefts, rights, up)

    up, down = ring_call(2, 0, rest, up_got, down_got, *gots)
    up_got, down_got = send(up, along_z(1)), send(down, along_z(-1))
    own, row_sum, *blocks = raw_second(keep, gain, gots, up, down)
    gots = [send(b, first_axis(o)) for b, o in zip(blocks, OFFSETS[1:])]

    up, down = ring_call(3, 2, rest, up_got, down_got, *gots)
    up_got, down_got = send(up, along_z(1)), send(down, along_z(-1))
    input_grad, gain_grad = raw_last(
        own, row_sum, gots, weight, inputs, cotangent, norm_gain, up, down
    )
    gain_grad = gain_grad + send(gain_grad, other_core)
    gain_grad = gain_grad + sum(send(gain_grad, xor_z(o)) for o in (1, 2, 3))

    sums, give = ring_last(spot, 4, rest, up_got, down_got, gain_grad)
    w_out_grad, w_in_grad = place(spot, sums, send(give, partner_y))
    (gain_grad,) = after([gain_grad], give)
    gain_grad = gain_grad + send(gain_grad, xor_z(4))
    return (input_grad, w_in_grad, w_out_grad.T, gain_grad[0])


def solution(mesh):
    in_specs = (
        P(("dp", "mp"), None),
        P(("dp", "mp"), None),
        P("dp", "mp"),
        P(),
        P(None, "mp"),
        P("mp", None),
    )
    out_specs = (P(("dp", "mp"), None), P("dp", "mp"), P("mp", "dp"), P())
    return jax.shard_map(body, mesh=mesh, in_specs=in_specs, out_specs=out_specs, check_vma=False)
```

```python
import functools
import math

import jax
import jax.numpy as jnp
from jax import lax
from jax.experimental import pallas as pl
from jax.experimental.pallas import tpu as pltpu
from jax.sharding import PartitionSpec as P

TOK_GROUP = 640
SEGS = 8
OWN = 40
ROW = 4 * OWN
CHUNK = 2 * ROW
PLANE = 4 * CHUNK
D = 1024
HID = 1024
PACK = 2 * D + 128
AXES = ("dp", "mp")
OFFSETS = (0, 1, -1, 2)
MIB = 1024 * 1024

GELU_C = 0.7978845608
GELU_A = 0.044715
F32, BF16 = jnp.float32, jnp.bfloat16


def coords(index):
    dp, mp = divmod(index, 16)
    return ((mp // 2) % 4, (mp // 8) * 2 + dp // 8, dp % 8, mp % 2)


def index_of(x, y, z, c):
    x, y, z = x % 4, y % 4, z % 8
    return ((y % 2) * 8 + z) * 16 + ((y // 2) * 4 + x) * 2 + c


def send(value, move):
    pairs = [(i, index_of(*move(*coords(i)))) for i in range(256)]
    return lax.ppermute(value, AXES, pairs)


def first_axis(o):
    return lambda x, y, z, c: (x + o, y, z, c) if c == 0 else (x, y + o, z, c)


def second_axis(o):
    return lambda x, y, z, c: (x, y + o, z, c) if c == 0 else (x + o, y, z, c)


def other_core(x, y, z, c):
    return (x, y, z, 1 - c)


def partner_y(x, y, z, c):
    return (x, y ^ 1, z, c)


def along_z(o):
    return lambda x, y, z, c: (x, y, z + o, c)


def xor_z(o):
    return lambda x, y, z, c: (x, y, z ^ o, c)


def params(mib):
    return pltpu.CompilerParams(vmem_limit_bytes=mib * MIB)


def cost(flops, moved, trans=0):
    return pl.CostEstimate(flops=flops, bytes_accessed=moved, transcendentals=trans)


def here(count):
    return [pl.BlockSpec(memory_space=pltpu.VMEM)] * count


def scalar():
    return pl.BlockSpec(memory_space=pltpu.SMEM)


def shape(*dims, dtype=BF16):
    return jax.ShapeDtypeStruct(dims, dtype)


def pack_kernel(spot_ref, x_hbm, cot_hbm, ids_hbm, gain_hbm, out_ref, x_ref, cot_ref, ids_ref, gain_ref, sems):
    copies = [
        pltpu.make_async_copy(src, dst, sems.at[k])
        for k, (src, dst) in enumerate(
            [(x_hbm, x_ref), (cot_hbm, cot_ref), (ids_hbm, ids_ref), (gain_hbm, gain_ref)]
        )
    ]
    for copy in copies:
        copy.start()
    for copy in copies:
        copy.wait()
    floats = x_ref[...].astype(F32)
    inv_rms = lax.rsqrt(jnp.mean(floats * floats, axis=-1, keepdims=True) + 1e-06)
    normed = floats * inv_rms
    out_ref[:, :D] = cot_ref[...]
    out_ref[:, D : 2 * D] = (normed * gain_ref[...].astype(F32).reshape(1, D)).astype(BF16)
    ids = jnp.broadcast_to((ids_ref[...] + SEGS * spot_ref[0]).astype(F32), (OWN, OWN))
    along = lax.broadcasted_iota(jnp.int32, (OWN, OWN), 0)
    across = lax.broadcasted_iota(jnp.int32, (OWN, OWN), 1)
    label = jnp.sum(jnp.where(along == across, ids, 0.0), axis=1, keepdims=True)
    out_ref[:, 2 * D :] = jnp.broadcast_to(label, (OWN, 128)).astype(BF16)


def pack(spot, inputs, cotangent, ids, gain):
    inputs_in_hbm = [
        pltpu.with_memory_space_constraint(a, pltpu.HBM) for a in (inputs, cotangent, ids, gain)
    ]
    return pl.pallas_call(
        pack_kernel,
        in_specs=[pl.BlockSpec(memory_space=pltpu.SMEM)]
        + [pl.BlockSpec(memory_space=pltpu.HBM)] * 4,
        out_shape=jax.ShapeDtypeStruct((OWN, PACK), BF16),
        scratch_shapes=[
            pltpu.VMEM((OWN, D), BF16),
            pltpu.VMEM((OWN, D), BF16),
            pltpu.VMEM((1, OWN), jnp.int32),
            pltpu.VMEM((D,), BF16),
            pltpu.SemaphoreType.DMA((4,)),
        ],
        compiler_params=params(4),
        cost_estimate=cost(OWN * D * 8, 4 * OWN * D * 2),
        name="pack_rows",
    )(spot, *inputs_in_hbm)


def nothing(*refs):
    pass


def after(values, *first):
    anywhere = pl.BlockSpec(memory_space=pl.ANY)
    return pl.pallas_call(
        nothing,
        in_specs=[anywhere] * (len(values) + len(first)),
        out_specs=[anywhere] * len(values),
        out_shape=[jax.ShapeDtypeStruct(v.shape, v.dtype) for v in values],
        input_output_aliases={k: k for k in range(len(values))},
        compiler_params=params(1),
        cost_estimate=cost(0, 0),
        name="after",
    )(*values, *first)


def relay_halves(plus, minus, *first):
    def kernel(plus_ref, minus_ref, *refs):
        refs[-2][...] = plus_ref[: ROW // 2, :]
        refs[-1][...] = minus_ref[ROW // 2 :, :]

    return pl.pallas_call(
        kernel,
        in_specs=here(2) + [pl.BlockSpec(memory_space=pl.ANY)] * len(first),
        out_specs=tuple(here(2)),
        out_shape=(shape(ROW // 2, PACK),) * 2,
        compiler_params=params(2),
        cost_estimate=cost(0, MIB),
        name="relay_halves",
    )(plus, minus, *first)


STEPS = 4
WIDTH = HID // STEPS


def chunk_kernel(count, *refs):
    srcs, (w_in_ref, w_out_ref) = refs[:count], refs[count : count + 2]
    left_ref, lab_ref, right_ref, mine_ref, theirs_ref, acc = refs[-6:]
    size = CHUNK // count
    for k, src in enumerate(srcs):
        rows = slice(k * size, (k + 1) * size)
        left_ref[rows, :] = src[:, : 2 * D]
        lab_ref[rows, :] = src[:, 2 * D :]
    for step in range(STEPS):
        cols = slice(step * WIDTH, (step + 1) * WIDTH)
        p = jnp.dot(left_ref[:, D:], w_in_ref[:, cols], preferred_element_type=F32)
        g = lax.dot_general(
            left_ref[:, :D], w_out_ref[cols, :], (((1,), (1,)), ((), ())), preferred_element_type=F32
        )
        p2 = p * p
        h = 0.5 * jnp.tanh(p * (GELU_C + (GELU_C * GELU_A) * p2)) + 0.5
        q = p * (2.0 * GELU_C + (6.0 * GELU_C * GELU_A) * p2)
        right_ref[:, cols] = (p * h).astype(BF16)
        pre_grad = (g * (h * (1.0 + (q - q * h)))).astype(BF16)
        right_ref[:, HID + step * WIDTH : HID + (step + 1) * WIDTH] = pre_grad
        raw = lax.dot_general(
            pre_grad, w_in_ref[:, cols], (((1,), (1,)), ((), ())), preferred_element_type=F32
        )
        if step == 0:
            acc[...] = raw
        elif step < STEPS - 1:
            acc[...] += raw
        else:
            mine_ref[...] = (acc[:ROW, :] + raw[:ROW]).astype(BF16)
            theirs_ref[...] = (acc[ROW:, :] + raw[ROW:]).astype(BF16)


def chunk(j, srcs, w_in, w_out, *first):
    shapes = [(CHUNK, 2 * D), (CHUNK, 128), (CHUNK, 2 * HID), (ROW, D), (ROW, D)]
    return pl.pallas_call(
        functools.partial(chunk_kernel, len(srcs)),
        in_specs=here(len(srcs) + 2) + [pl.BlockSpec(memory_space=pl.ANY)] * len(first),
        out_specs=here(5),
        scratch_shapes=[pltpu.VMEM((CHUNK, D), F32)],
        out_shape=[shape(*s) for s in shapes],
        compiler_params=params(8),
        cost_estimate=cost(6 * CHUNK * D * HID, 9 * MIB, CHUNK * HID),
        name="chunk_%d" % j,
    )(*srcs, w_in, w_out, *first)


def token_weights(labels):
    labels = labels.astype(F32)
    lanes = lax.broadcasted_iota(jnp.int32, (PLANE, 128), 1).astype(F32)
    onehot = jnp.where(labels == lanes, 1.0, 0.0)
    counts = jnp.sum(onehot, axis=0, keepdims=True)
    token_count = jnp.sum(onehot * counts, axis=1, keepdims=True)
    weights = jnp.sqrt(TOK_GROUP / (SEGS * token_count))
    padding = jnp.sum(onehot * jnp.where((lanes == 7.0) | (lanes == 15.0), 1.0, 0.0), axis=1, keepdims=True)
    return jnp.where(padding > 0.5, 0.0, weights)


GRAD_SCALE = 1.0 / math.sqrt(TOK_GROUP * 16)


RIDE = 16


def fold(row):
    return jnp.concatenate([row[:, k * 128 : (k + 1) * 128] for k in range(8)], axis=0)


def unfold(block):
    return jnp.concatenate([block[k : k + 1, :] for k in range(8)], axis=1)


def gain_call(weight, lefts, raws, *first):
    def kernel(w_ref, *refs):
        lefts, raws, gain_ref = refs[:4], refs[4:12], refs[-1]
        total = jnp.zeros((1, D), F32)
        for k, raw in enumerate(raws):
            rows = slice((k % 2) * ROW, (k % 2 + 1) * ROW)
            w = w_ref[k * ROW : (k + 1) * ROW, :1]
            term = lefts[k // 2][rows, D:].astype(F32) * raw[...].astype(F32) * w
            total = total + jnp.sum(term, axis=0, keepdims=True)
        gain_ref[...] = fold(total)

    anywhere = pl.BlockSpec(memory_space=pl.ANY)
    return pl.pallas_call(
        kernel,
        in_specs=here(13) + [anywhere] * len(first),
        out_shape=shape(8, 128, dtype=F32),
        compiler_params=params(8),
        cost_estimate=cost(4 * PLANE * D, 8 * MIB),
        name="gain_term",
    )(weight, *lefts, *raws, *first)


def term_block(array, offsets, z, weight, lefts, rights):
    lane = lax.broadcasted_iota(jnp.int32, (PLANE, 128), 1)
    blocks = []
    for offset in offsets:
        to = lax.rem(z + offset + 8, 8)
        shift = lax.rem(to, 2) * 64
        halves = []
        for y in range(2):
            start = pl.multiple_of(array * D + y * (D // 2) + (to // 2) * 128, 128)
            left = jnp.concatenate([ref[:, pl.ds(start, 128)] for ref in lefts], axis=0).astype(F32)
            halves.append(pltpu.roll(left * weight, shift if y == 0 else 64 - shift, 1))
        blocks.append(jnp.where(lane < 64, *halves).astype(BF16))
    left = jnp.concatenate(blocks, axis=1)
    right = jnp.concatenate([ref[:, array * HID : (array + 1) * HID] for ref in rights], axis=0)
    total = lax.dot_general(left, right, (((0,), (0,)), ((), ())), preferred_element_type=F32)
    return (total * GRAD_SCALE).astype(BF16)


def far_call(spot, labs, lefts, rights, theirs):
    def kernel(spot_ref, *refs):
        labs, lefts, rights, theirs = refs[:4], refs[4:8], refs[8:12], refs[12:16]
        weight_ref, up_ref, down_ref, theirs_ref = refs[16:]
        weights = token_weights(jnp.concatenate([lab[...] for lab in labs], axis=0))
        weight_ref[...] = jnp.broadcast_to(weights, (PLANE, 128))
        for array, ref in enumerate((up_ref, down_ref)):
            block = term_block(array, (4,), spot_ref[1], weight_ref[...], lefts, rights)
            ref[...] = block.reshape(2, 64, HID)
        for j, raw in enumerate(theirs):
            theirs_ref[j * ROW : (j + 1) * ROW, :] = raw[...]

    return pl.pallas_call(
        kernel,
        in_specs=[scalar()] + here(16),
        out_specs=tuple(here(4)),
        out_shape=(
            shape(PLANE, 128, dtype=F32),
            shape(2, 64, HID),
            shape(2, 64, HID),
            shape(TOK_GROUP, D),
        ),
        compiler_params=params(12),
        cost_estimate=cost(PLANE * D * HID, 8 * MIB),
        name="far_terms",
    )(spot, *labs, *lefts, *rights, *theirs)


def terms_call(name, groups, spot, weight, lefts, rights, *first):
    count = sum(len(group) for group in groups)

    def kernel(spot_ref, weight_ref, *refs):
        lefts, rights, out_ref = refs[:4], refs[4:8], refs[-1]
        at = 0
        for group in groups:
            for array in range(2):
                block = term_block(array, group, spot_ref[1], weight_ref[...], lefts, rights)
                block = block.reshape(len(group), 2, 64, HID)
                for k in range(len(group)):
                    out_ref[at + k, array] = block[k]
            at += len(group)

    return pl.pallas_call(
        kernel,
        in_specs=[scalar()] + here(9) + [pl.BlockSpec(memory_space=pl.ANY)] * len(first),
        out_specs=here(1)[0],
        out_shape=shape(count, 2, 2, 64, HID),
        compiler_params=params(12),
        cost_estimate=cost(count * PLANE * 512 * HID, 8 * MIB),
        name=name,
    )(spot, weight, *lefts, *rights, *first)


def add(*terms):
    return sum(t.astype(F32) for t in terms).astype(BF16)


def ring_call(step, at, terms, plus, minus, *first):
    def kernel(terms_ref, plus_ref, minus_ref, *refs):
        up_ref, down_ref = refs[-2:]
        if step == 1:
            up_ref[0] = add(plus_ref[...], terms_ref[at, 0])
            up_ref[1] = terms_ref[at, 1]
            down_ref[0] = terms_ref[at + 1, 0]
            down_ref[1] = add(minus_ref[...], terms_ref[at + 1, 1])
        else:
            for array in range(2):
                up_ref[array] = add(plus_ref[array], terms_ref[at, array])
                down_ref[array] = add(minus_ref[array], terms_ref[at + 1, array])

    anywhere = pl.BlockSpec(memory_space=pl.ANY)
    return pl.pallas_call(
        kernel,
        in_specs=here(3) + [anywhere] * len(first),
        out_specs=tuple(here(2)),
        out_shape=(shape(2, 2, 64, HID),) * 2,
        compiler_params=params(4),
        cost_estimate=cost(4 * MIB, 4 * MIB),
        name="ring_%d" % step,
    )(terms, plus, minus, *first)


def ring_last(spot, at, terms, plus, minus, *first):
    def kernel(spot_ref, terms_ref, plus_ref, minus_ref, *refs):
        mine_ref, give_ref = refs[-2:]
        own = spot_ref[0]
        for array in range(2):
            for ref, y in ((give_ref, 1 - own), (mine_ref, own)):
                ref[array] = add(terms_ref[at, array, y], plus_ref[array, y], minus_ref[array, y])

    anywhere = pl.BlockSpec(memory_space=pl.ANY)
    return pl.pallas_call(
        kernel,
        in_specs=[scalar()] + here(3) + [anywhere] * len(first),
        out_specs=tuple(here(2)),
        out_shape=(shape(2, 64, HID),) * 2,
        compiler_params=params(4),
        cost_estimate=cost(MIB, 2 * MIB),
        name="ring_last",
    )(spot, terms, plus, minus, *first)


def place(other, spot, half, *outs):
    olds = outs if other else ()

    def kernel(spot_ref, half_ref, *refs):
        for array, out in enumerate(refs[-2:]):
            out[...] = half_ref[array]

    column = pl.BlockSpec((64, HID), lambda i, spot: (0, spot[0] ^ other))
    anywhere = [pl.BlockSpec(memory_space=pl.ANY)]
    return pl.pallas_call(
        kernel,
        grid_spec=pltpu.PrefetchScalarGridSpec(
            num_scalar_prefetch=1,
            grid=(1,),
            in_specs=here(1) + anywhere * len(outs),
            out_specs=(column,) * 2,
        ),
        out_shape=(pltpu.HBM((64, 2 * HID), BF16),) * 2,
        input_output_aliases={2 + k: k for k in range(len(olds))},
        compiler_params=params(4),
        cost_estimate=cost(MIB, MIB),
        name="place_%d" % other,
    )(spot, half, *outs)


def ride_rows(total):
    high = total.astype(BF16).astype(F32)
    rows = lax.broadcasted_iota(jnp.int32, (RIDE, D), 0)
    return jnp.where(rows == 0, high, jnp.where(rows == 1, total - high, 0.0)).astype(BF16)


def ride_sum(rows):
    return jnp.sum(rows.astype(F32), axis=0, keepdims=True)


def raw_first(mine, got, gain, *first):
    def kernel(*refs):
        mines, got_ref, gain_ref = refs[:4], refs[4], refs[5]
        keep_ref, *sends = refs[-4:]
        keep_ref[...] = mines[0][...].astype(F32) + got_ref[:ROW, :].astype(F32)
        ride = ride_rows(unfold(gain_ref[...]))
        for j in range(1, 4):
            sends[j - 1][:ROW, :] = add(mines[j][...], got_ref[j * ROW : (j + 1) * ROW, :])
            sends[j - 1][ROW:, :] = ride

    anywhere = pl.BlockSpec(memory_space=pl.ANY)
    return pl.pallas_call(
        kernel,
        in_specs=here(6) + [anywhere] * len(first),
        out_specs=tuple(here(4)),
        out_shape=(shape(ROW, D, dtype=F32),) + (shape(ROW + RIDE, D),) * 3,
        compiler_params=params(4),
        cost_estimate=cost(2 * MIB, 4 * MIB),
        name="raw_first",
    )(*mine, got, gain, *first)


def raw_second(keep, gain, gots, *first):
    def kernel(keep_ref, gain_ref, *refs):
        gots = refs[:3]
        mine_ref, total_ref, *sends = refs[-5:]
        total = keep_ref[...]
        row = ride_sum(ride_rows(unfold(gain_ref[...])))
        for got in gots:
            total = total + got[:ROW, :].astype(F32)
            row = row + ride_sum(got[ROW:, :])
        ride = ride_rows(row)
        mine_ref[...] = total[:OWN]
        total_ref[...] = jnp.broadcast_to(ride_sum(ride), (8, D))
        for j in range(1, 4):
            block = jnp.concatenate([total[j * OWN : (j + 1) * OWN], jnp.zeros((8, D), F32)], axis=0)
            sends[j - 1][: OWN + 8, :] = block.astype(BF16)
            sends[j - 1][OWN + 8 :, :] = ride

    anywhere = pl.BlockSpec(memory_space=pl.ANY)
    return pl.pallas_call(
        kernel,
        in_specs=here(5) + [anywhere] * len(first),
        out_specs=tuple(here(5)),
        out_shape=(shape(OWN, D, dtype=F32), shape(8, D, dtype=F32))
        + (shape(OWN + 8 + RIDE, D),) * 3,
        compiler_params=params(6),
        cost_estimate=cost(2 * MIB, 2 * MIB),
        name="raw_second",
    )(keep, gain, *gots, *first)


def raw_last(mine, row, gots, weight, inputs, cotangent, gain, *first):
    def kernel(mine_ref, row_ref, *refs):
        gots, (w_ref, x_ref, cot_ref, gain_ref), (grad_ref, gain_out) = refs[:3], refs[3:7], refs[-2:]
        raw, row = mine_ref[...], row_ref[:1, :]
        for got in gots:
            raw = raw + got[: OWN + 8, :].astype(F32)[:OWN]
            row = row + ride_sum(got[OWN + 8 :, :])
        gain = gain_ref[...].astype(F32).reshape(1, D)
        gain_out[...] = fold(row / gain)
        w = w_ref[:OWN, :1]
        floats = x_ref[...].astype(F32)
        inv_rms = lax.rsqrt(jnp.mean(floats * floats, axis=-1, keepdims=True) + 1e-06)
        normed = floats * inv_rms
        dn = raw * w * gain
        inner = jnp.mean(dn * normed, axis=-1, keepdims=True)
        ge = (cot_ref[...].astype(F32) * w).astype(BF16).astype(F32)
        grad_ref[...] = (ge + inv_rms * (dn - normed * inner)).astype(BF16)

    return pl.pallas_call(
        kernel,
        in_specs=here(9) + [pl.BlockSpec(memory_space=pl.ANY)] * len(first),
        out_specs=tuple(here(2)),
        out_shape=(shape(OWN, D), shape(8, 128, dtype=F32)),
        compiler_params=params(4),
        cost_estimate=cost(MIB, MIB),
        name="raw_last",
    )(mine, row, *gots, weight, inputs, cotangent, gain, *first)


def body(inputs, cotangent, segment_ids, norm_gain, w_in, w_out):
    dp = lax.axis_index("dp")
    y_lo, z = lax.div(dp, 8), lax.rem(dp, 8)
    spot = jnp.stack([y_lo, z])
    packed = pack(spot, inputs, cotangent, segment_ids, norm_gain)

    row = jnp.concatenate([packed] + [send(packed, first_axis(-o)) for o in OFFSETS[1:]], axis=0)
    w_in = lax.dynamic_slice_in_dim(w_in, y_lo * HID, HID, 1)
    w_out = lax.dynamic_slice_in_dim(w_out, y_lo * HID, HID, 0)
    (row,) = after([row], w_in, w_out)
    plus, minus = send(row, second_axis(-1)), send(row, second_axis(1))
    parts = [chunk(0, [row, send(row, other_core)], w_in, w_out)]
    plus, minus = after([plus, minus], parts[0][1])
    relayed = [
        send(part, second_axis(o)) for part, o in zip(relay_halves(plus, minus), (-1, 1))
    ]
    parts.append(chunk(1, [plus, send(plus, other_core)], w_in, w_out))
    swapped = send(minus, other_core)
    parts.append(chunk(2, [minus, swapped], w_in, w_out, parts[1][1]))
    relayed = after(relayed, parts[2][1])
    parts.append(chunk(3, [*relayed, *(send(r, other_core) for r in relayed)], w_in, w_out))
    lefts, labs, rights, mine, theirs = zip(*parts)

    weight, up, down, theirs_all = far_call(spot, labs, lefts, rights, theirs)
    up_got, down_got = send(up, along_z(1)), send(down, along_z(-1))
    raw_got = send(theirs_all, other_core)
    raws = [raw for pair in zip(mine, theirs) for raw in pair]
    gain = gain_call(weight, lefts, raws)
    gain_got = send(gain, other_core)
    near = terms_call("near_terms", [(3, -3)], spot, weight, lefts, rights, gain)
    gain = gain + gain_got
    gain = gain + send(gain, xor_z(1))
    keep, *blocks = raw_first(mine, raw_got, gain, near)
    gots = [send(b, second_axis(o)) for b, o in zip(blocks, OFFSETS[1:])]

    up, down = ring_call(1, 0, near, up_got, down_got, *blocks)
    up_got, down_got = send(up, along_z(1)), send(down, along_z(-1))
    middle = terms_call("middle_terms", [(2, -2)], spot, weight, lefts, rights, up)

    up, down = ring_call(2, 0, middle, up_got, down_got, *gots)
    up_got, down_got = send(up, along_z(1)), send(down, along_z(-1))
    rest = terms_call("rest_terms", [(1, -1), (0,)], spot, weight, lefts, rights, up)
    own, row_sum, *blocks = raw_second(keep, gain, gots, up, down)
    gots = [send(b, first_axis(o)) for b, o in zip(blocks, OFFSETS[1:])]

    up, down = ring_call(3, 0, rest, up_got, down_got, *gots)
    up_got, down_got = send(up, along_z(1)), send(down, along_z(-1))
    input_grad, gain_grad = raw_last(
        own, row_sum, gots, weight, inputs, cotangent, norm_gain, up, down
    )
    gain_grad = gain_grad + sum(send(gain_grad, xor_z(o)) for o in (2, 4, 6))

    sums, give = ring_last(spot, 2, rest, up_got, down_got, gain_grad)
    outs = place(0, spot, sums, give)
    w_out_grad, w_in_grad = place(1, spot, send(give, partner_y), *outs)
    return (input_grad, w_in_grad, w_out_grad.T, gain_grad.reshape(D))


def solution(mesh):
    in_specs = (
        P(("dp", "mp"), None),
        P(("dp", "mp"), None),
        P("dp", "mp"),
        P(),
        P(None, "mp"),
        P("mp", None),
    )
    out_specs = (P(("dp", "mp"), None), P("dp", "mp"), P("mp", "dp"), P())
    return jax.shard_map(body, mesh=mesh, in_specs=in_specs, out_specs=out_specs, check_vma=False)
```

```python
import functools
import math

import jax
import jax.numpy as jnp
from jax import lax
from jax.experimental import pallas as pl
from jax.experimental.pallas import tpu as pltpu
from jax.sharding import PartitionSpec as P

TOK_GROUP = 640
SEGS = 8
OWN = 40
ROW = 4 * OWN
CHUNK = 2 * ROW
PLANE = 4 * CHUNK
D = 1024
HID = 1024
PACK = 2 * D + 128
AXES = ("dp", "mp")
OFFSETS = (0, 1, -1, 2)
MIB = 1024 * 1024

GELU_C = 0.7978845608
GELU_A = 0.044715
F32, BF16 = jnp.float32, jnp.bfloat16


def coords(index):
    dp, mp = divmod(index, 16)
    return ((mp // 2) % 4, (mp // 8) * 2 + dp // 8, dp % 8, mp % 2)


def index_of(x, y, z, c):
    x, y, z = x % 4, y % 4, z % 8
    return ((y % 2) * 8 + z) * 16 + ((y // 2) * 4 + x) * 2 + c


def send(value, move):
    pairs = [(i, index_of(*move(*coords(i)))) for i in range(256)]
    return lax.ppermute(value, AXES, pairs)


def first_axis(o):
    return lambda x, y, z, c: (x + o, y, z, c) if c == 0 else (x, y + o, z, c)


def second_axis(o):
    return lambda x, y, z, c: (x, y + o, z, c) if c == 0 else (x + o, y, z, c)


def other_core(x, y, z, c):
    return (x, y, z, 1 - c)


def partner_y(x, y, z, c):
    return (x, y ^ 1, z, c)


def along_z(o):
    return lambda x, y, z, c: (x, y, z + o, c)


def xor_z(o):
    return lambda x, y, z, c: (x, y, z ^ o, c)


def params(mib):
    return pltpu.CompilerParams(vmem_limit_bytes=mib * MIB)


def cost(flops, moved, trans=0):
    return pl.CostEstimate(flops=flops, bytes_accessed=moved, transcendentals=trans)


def here(count):
    return [pl.BlockSpec(memory_space=pltpu.VMEM)] * count


def scalar():
    return pl.BlockSpec(memory_space=pltpu.SMEM)


def shape(*dims, dtype=BF16):
    return jax.ShapeDtypeStruct(dims, dtype)


def pack_kernel(spot_ref, x_hbm, cot_hbm, ids_hbm, gain_hbm, out_ref, x_ref, cot_ref, ids_ref, gain_ref, sems):
    copies = [
        pltpu.make_async_copy(src, dst, sems.at[k])
        for k, (src, dst) in enumerate(
            [(x_hbm, x_ref), (cot_hbm, cot_ref), (ids_hbm, ids_ref), (gain_hbm, gain_ref)]
        )
    ]
    for copy in copies:
        copy.start()
    for copy in copies:
        copy.wait()
    floats = x_ref[...].astype(F32)
    inv_rms = lax.rsqrt(jnp.mean(floats * floats, axis=-1, keepdims=True) + 1e-06)
    normed = floats * inv_rms
    out_ref[:, :D] = cot_ref[...]
    out_ref[:, D : 2 * D] = (normed * gain_ref[...].astype(F32).reshape(1, D)).astype(BF16)
    ids = jnp.broadcast_to((ids_ref[...] + SEGS * spot_ref[0]).astype(F32), (OWN, OWN))
    along = lax.broadcasted_iota(jnp.int32, (OWN, OWN), 0)
    across = lax.broadcasted_iota(jnp.int32, (OWN, OWN), 1)
    label = jnp.sum(jnp.where(along == across, ids, 0.0), axis=1, keepdims=True)
    out_ref[:, 2 * D :] = jnp.broadcast_to(label, (OWN, 128)).astype(BF16)


def pack(spot, inputs, cotangent, ids, gain):
    inputs_in_hbm = [
        pltpu.with_memory_space_constraint(a, pltpu.HBM) for a in (inputs, cotangent, ids, gain)
    ]
    return pl.pallas_call(
        pack_kernel,
        in_specs=[pl.BlockSpec(memory_space=pltpu.SMEM)]
        + [pl.BlockSpec(memory_space=pltpu.HBM)] * 4,
        out_shape=jax.ShapeDtypeStruct((OWN, PACK), BF16),
        scratch_shapes=[
            pltpu.VMEM((OWN, D), BF16),
            pltpu.VMEM((OWN, D), BF16),
            pltpu.VMEM((1, OWN), jnp.int32),
            pltpu.VMEM((D,), BF16),
            pltpu.SemaphoreType.DMA((4,)),
        ],
        compiler_params=params(4),
        cost_estimate=cost(OWN * D * 8, 4 * OWN * D * 2),
        name="pack_rows",
    )(spot, *inputs_in_hbm)


def nothing(*refs):
    pass


def after(values, *first):
    anywhere = pl.BlockSpec(memory_space=pl.ANY)
    return pl.pallas_call(
        nothing,
        in_specs=[anywhere] * (len(values) + len(first)),
        out_specs=[anywhere] * len(values),
        out_shape=[jax.ShapeDtypeStruct(v.shape, v.dtype) for v in values],
        input_output_aliases={k: k for k in range(len(values))},
        compiler_params=params(1),
        cost_estimate=cost(0, 0),
        name="after",
    )(*values, *first)


def copied(value, *first):
    def kernel(value_ref, *refs):
        refs[-1][...] = value_ref[...]

    return pl.pallas_call(
        kernel,
        in_specs=here(1) + [pl.BlockSpec(memory_space=pl.ANY)] * len(first),
        out_specs=here(1)[0],
        out_shape=shape(*value.shape),
        compiler_params=params(2),
        cost_estimate=cost(0, MIB),
        name="copied",
    )(value, *first)


def relay_halves(plus, minus, *first):
    def kernel(plus_ref, minus_ref, *refs):
        refs[-2][...] = plus_ref[: ROW // 2, :]
        refs[-1][...] = minus_ref[ROW // 2 :, :]

    return pl.pallas_call(
        kernel,
        in_specs=here(2) + [pl.BlockSpec(memory_space=pl.ANY)] * len(first),
        out_specs=tuple(here(2)),
        out_shape=(shape(ROW // 2, PACK),) * 2,
        compiler_params=params(2),
        cost_estimate=cost(0, MIB),
        name="relay_halves",
    )(plus, minus, *first)


STEPS = 4
WIDTH = HID // STEPS


def chunk_kernel(count, *refs):
    srcs, (w_in_ref, w_out_ref) = refs[:count], refs[count : count + 2]
    left_ref, lab_ref, right_ref, mine_ref, theirs_ref, acc = refs[-6:]
    size = CHUNK // count
    for k, src in enumerate(srcs):
        rows = slice(k * size, (k + 1) * size)
        left_ref[rows, :] = src[:, : 2 * D]
        lab_ref[rows, :] = src[:, 2 * D :]
    for step in range(STEPS):
        cols = slice(step * WIDTH, (step + 1) * WIDTH)
        p = jnp.dot(left_ref[:, D:], w_in_ref[:, cols], preferred_element_type=F32)
        g = lax.dot_general(
            left_ref[:, :D], w_out_ref[cols, :], (((1,), (1,)), ((), ())), preferred_element_type=F32
        )
        p2 = p * p
        h = 0.5 * jnp.tanh(p * (GELU_C + (GELU_C * GELU_A) * p2)) + 0.5
        q = p * (2.0 * GELU_C + (6.0 * GELU_C * GELU_A) * p2)
        right_ref[:, cols] = (p * h).astype(BF16)
        pre_grad = (g * (h * (1.0 + (q - q * h)))).astype(BF16)
        right_ref[:, HID + step * WIDTH : HID + (step + 1) * WIDTH] = pre_grad
        raw = lax.dot_general(
            pre_grad, w_in_ref[:, cols], (((1,), (1,)), ((), ())), preferred_element_type=F32
        )
        if step == 0:
            acc[...] = raw
        elif step < STEPS - 1:
            acc[...] += raw
        else:
            mine_ref[...] = (acc[:ROW, :] + raw[:ROW]).astype(BF16)
            theirs_ref[...] = (acc[ROW:, :] + raw[ROW:]).astype(BF16)


def chunk(j, srcs, w_in, w_out, *first):
    shapes = [(CHUNK, 2 * D), (CHUNK, 128), (CHUNK, 2 * HID), (ROW, D), (ROW, D)]
    return pl.pallas_call(
        functools.partial(chunk_kernel, len(srcs)),
        in_specs=here(len(srcs) + 2) + [pl.BlockSpec(memory_space=pl.ANY)] * len(first),
        out_specs=here(5),
        scratch_shapes=[pltpu.VMEM((CHUNK, D), F32)],
        out_shape=[shape(*s) for s in shapes],
        compiler_params=params(8),
        cost_estimate=cost(6 * CHUNK * D * HID, 9 * MIB, CHUNK * HID),
        name="chunk_%d" % j,
    )(*srcs, w_in, w_out, *first)


def token_weights(labels):
    labels = labels.astype(F32)
    lanes = lax.broadcasted_iota(jnp.int32, (PLANE, 128), 1).astype(F32)
    onehot = jnp.where(labels == lanes, 1.0, 0.0)
    counts = jnp.sum(onehot, axis=0, keepdims=True)
    token_count = jnp.sum(onehot * counts, axis=1, keepdims=True)
    weights = jnp.sqrt(TOK_GROUP / (SEGS * token_count))
    padding = jnp.sum(onehot * jnp.where((lanes == 7.0) | (lanes == 15.0), 1.0, 0.0), axis=1, keepdims=True)
    return jnp.where(padding > 0.5, 0.0, weights)


GRAD_SCALE = 1.0 / math.sqrt(TOK_GROUP * 16)


RIDE = 16


def fold(row):
    return jnp.concatenate([row[:, k * 128 : (k + 1) * 128] for k in range(8)], axis=0)


def unfold(block):
    return jnp.concatenate([block[k : k + 1, :] for k in range(8)], axis=1)


def gain_call(weight, lefts, raws, *first):
    def kernel(w_ref, *refs):
        lefts, raws, gain_ref = refs[:4], refs[4:12], refs[-1]
        total = jnp.zeros((1, D), F32)
        for k, raw in enumerate(raws):
            rows = slice((k % 2) * ROW, (k % 2 + 1) * ROW)
            w = w_ref[k * ROW : (k + 1) * ROW, :1]
            term = lefts[k // 2][rows, D:].astype(F32) * raw[...].astype(F32) * w
            total = total + jnp.sum(term, axis=0, keepdims=True)
        gain_ref[...] = fold(total)

    anywhere = pl.BlockSpec(memory_space=pl.ANY)
    return pl.pallas_call(
        kernel,
        in_specs=here(13) + [anywhere] * len(first),
        out_shape=shape(8, 128, dtype=F32),
        compiler_params=params(8),
        cost_estimate=cost(4 * PLANE * D, 8 * MIB),
        name="gain_term",
    )(weight, *lefts, *raws, *first)


def term_block(array, offsets, z, weight, lefts, rights):
    low = (lax.broadcasted_iota(jnp.int32, (PLANE, 128), 1) < 64).astype(jnp.int32)
    blocks = []
    for offset in offsets:
        to = lax.rem(z + offset + 8, 8)
        odd = lax.rem(to, 2)
        start = array * D + (to // 2) * 128
        moved, kept = (
            jnp.concatenate([ref[:, pl.ds(pl.multiple_of(at, 128), 128)] for ref in lefts], axis=0)
            for at in (start + (1 - odd) * (D // 2), start + odd * (D // 2))
        )
        moved = pltpu.roll(moved.astype(F32), 64, 1)
        blocks.append((jnp.where(low == odd, moved, kept.astype(F32)) * weight).astype(BF16))
    left = jnp.concatenate(blocks, axis=1)
    right = jnp.concatenate([ref[:, array * HID : (array + 1) * HID] for ref in rights], axis=0)
    total = lax.dot_general(left, right, (((0,), (0,)), ((), ())), preferred_element_type=F32)
    return (total * GRAD_SCALE).astype(BF16)


def far_call(spot, labs, lefts, rights, theirs):
    def kernel(spot_ref, *refs):
        labs, lefts, rights, theirs = refs[:4], refs[4:8], refs[8:12], refs[12:16]
        weight_ref, up_ref, down_ref, theirs_ref = refs[16:]
        weights = token_weights(jnp.concatenate([lab[...] for lab in labs], axis=0))
        weight_ref[...] = jnp.broadcast_to(weights, (PLANE, 128))
        for array, ref in enumerate((up_ref, down_ref)):
            block = term_block(array, (4,), spot_ref[1], weight_ref[...], lefts, rights)
            ref[...] = block.reshape(2, 64, HID)
        for j, raw in enumerate(theirs):
            theirs_ref[j * ROW : (j + 1) * ROW, :] = raw[...]

    return pl.pallas_call(
        kernel,
        in_specs=[scalar()] + here(16),
        out_specs=tuple(here(4)),
        out_shape=(
            shape(PLANE, 128, dtype=F32),
            shape(2, 64, HID),
            shape(2, 64, HID),
            shape(TOK_GROUP, D),
        ),
        compiler_params=params(12),
        cost_estimate=cost(PLANE * D * HID, 8 * MIB),
        name="far_terms",
    )(spot, *labs, *lefts, *rights, *theirs)


def terms_call(name, groups, spot, weight, lefts, rights, *first):
    count = sum(len(group) for group in groups)

    def kernel(spot_ref, weight_ref, *refs):
        lefts, rights, out_ref = refs[:4], refs[4:8], refs[-1]
        at = 0
        for group in groups:
            for array in range(2):
                block = term_block(array, group, spot_ref[1], weight_ref[...], lefts, rights)
                block = block.reshape(len(group), 2, 64, HID)
                for k in range(len(group)):
                    out_ref[at + k, array] = block[k]
            at += len(group)

    return pl.pallas_call(
        kernel,
        in_specs=[scalar()] + here(9) + [pl.BlockSpec(memory_space=pl.ANY)] * len(first),
        out_specs=here(1)[0],
        out_shape=shape(count, 2, 2, 64, HID),
        compiler_params=params(12),
        cost_estimate=cost(count * PLANE * 512 * HID, 8 * MIB),
        name=name,
    )(spot, weight, *lefts, *rights, *first)


def add(*terms):
    return sum(t.astype(F32) for t in terms).astype(BF16)


def ring_call(step, at, terms, plus, minus, *first):
    def kernel(terms_ref, plus_ref, minus_ref, *refs):
        up_ref, down_ref = refs[-2:]
        if step == 1:
            up_ref[0] = add(plus_ref[...], terms_ref[at, 0])
            up_ref[1] = terms_ref[at, 1]
            down_ref[0] = terms_ref[at + 1, 0]
            down_ref[1] = add(minus_ref[...], terms_ref[at + 1, 1])
        else:
            for array in range(2):
                up_ref[array] = add(plus_ref[array], terms_ref[at, array])
                down_ref[array] = add(minus_ref[array], terms_ref[at + 1, array])

    anywhere = pl.BlockSpec(memory_space=pl.ANY)
    return pl.pallas_call(
        kernel,
        in_specs=here(3) + [anywhere] * len(first),
        out_specs=tuple(here(2)),
        out_shape=(shape(2, 2, 64, HID),) * 2,
        compiler_params=params(4),
        cost_estimate=cost(4 * MIB, 4 * MIB),
        name="ring_%d" % step,
    )(terms, plus, minus, *first)


def ring_last(spot, at, terms, plus, minus, *first):
    def kernel(spot_ref, terms_ref, plus_ref, minus_ref, *refs):
        mine_ref, give_ref = refs[-2:]
        own = spot_ref[0]
        for array in range(2):
            for ref, y in ((give_ref, 1 - own), (mine_ref, own)):
                ref[array] = add(terms_ref[at, array, y], plus_ref[array, y], minus_ref[array, y])

    anywhere = pl.BlockSpec(memory_space=pl.ANY)
    return pl.pallas_call(
        kernel,
        in_specs=[scalar()] + here(3) + [anywhere] * len(first),
        out_specs=tuple(here(2)),
        out_shape=(shape(2, 64, HID),) * 2,
        compiler_params=params(4),
        cost_estimate=cost(MIB, 2 * MIB),
        name="ring_last",
    )(spot, terms, plus, minus, *first)


def place(other, spot, half, *outs):
    olds = outs if other else ()

    def kernel(spot_ref, half_ref, *refs):
        *_, first, second, sems = refs
        column = spot_ref[0] if other == 0 else 1 - spot_ref[0]
        cols = pl.ds(pl.multiple_of(column * HID, HID), HID)
        copies = [
            pltpu.make_async_copy(half_ref.at[array], out.at[:, cols], sems.at[array])
            for array, out in enumerate((first, second))
        ]
        for copy in copies:
            copy.start()
        for copy in copies:
            copy.wait()

    anywhere = [pl.BlockSpec(memory_space=pl.ANY)]
    return pl.pallas_call(
        kernel,
        in_specs=[scalar()] + here(1) + anywhere * len(outs),
        out_specs=(pl.BlockSpec(memory_space=pltpu.HBM),) * 2,
        out_shape=(pltpu.HBM((64, 2 * HID), BF16),) * 2,
        scratch_shapes=[pltpu.SemaphoreType.DMA((2,))],
        input_output_aliases={2 + k: k for k in range(len(olds))},
        compiler_params=params(4),
        cost_estimate=cost(MIB, MIB),
        name="place_%d" % other,
    )(spot, half, *outs)


def ride_rows(total):
    high = total.astype(BF16).astype(F32)
    rows = lax.broadcasted_iota(jnp.int32, (RIDE, D), 0)
    return jnp.where(rows == 0, high, jnp.where(rows == 1, total - high, 0.0)).astype(BF16)


def ride_sum(rows):
    return jnp.sum(rows.astype(F32), axis=0, keepdims=True)


def raw_first(mine, got, gain, *first):
    def kernel(*refs):
        mines, got_ref, gain_ref = refs[:4], refs[4], refs[5]
        keep_ref, *sends = refs[-4:]
        keep_ref[...] = mines[0][...].astype(F32) + got_ref[:ROW, :].astype(F32)
        ride = ride_rows(unfold(gain_ref[...]))
        for j in range(1, 4):
            sends[j - 1][:ROW, :] = add(mines[j][...], got_ref[j * ROW : (j + 1) * ROW, :])
            sends[j - 1][ROW:, :] = ride

    anywhere = pl.BlockSpec(memory_space=pl.ANY)
    return pl.pallas_call(
        kernel,
        in_specs=here(6) + [anywhere] * len(first),
        out_specs=tuple(here(4)),
        out_shape=(shape(ROW, D, dtype=F32),) + (shape(ROW + RIDE, D),) * 3,
        compiler_params=params(4),
        cost_estimate=cost(2 * MIB, 4 * MIB),
        name="raw_first",
    )(*mine, got, gain, *first)


def raw_second(keep, gain, gots, *first):
    def kernel(keep_ref, gain_ref, *refs):
        gots = refs[:3]
        mine_ref, total_ref, *sends = refs[-5:]
        total = keep_ref[...]
        row = ride_sum(ride_rows(unfold(gain_ref[...])))
        for got in gots:
            total = total + got[:ROW, :].astype(F32)
            row = row + ride_sum(got[ROW:, :])
        ride = ride_rows(row)
        mine_ref[...] = total[:OWN]
        total_ref[...] = jnp.broadcast_to(ride_sum(ride), (8, D))
        for j in range(1, 4):
            block = jnp.concatenate([total[j * OWN : (j + 1) * OWN], jnp.zeros((8, D), F32)], axis=0)
            sends[j - 1][: OWN + 8, :] = block.astype(BF16)
            sends[j - 1][OWN + 8 :, :] = ride

    anywhere = pl.BlockSpec(memory_space=pl.ANY)
    return pl.pallas_call(
        kernel,
        in_specs=here(5) + [anywhere] * len(first),
        out_specs=tuple(here(5)),
        out_shape=(shape(OWN, D, dtype=F32), shape(8, D, dtype=F32))
        + (shape(OWN + 8 + RIDE, D),) * 3,
        compiler_params=params(6),
        cost_estimate=cost(2 * MIB, 2 * MIB),
        name="raw_second",
    )(keep, gain, *gots, *first)


def raw_last(mine, row, gots, weight, inputs, cotangent, gain, *first):
    def kernel(mine_ref, row_ref, *refs):
        gots, (w_ref, x_ref, cot_ref, gain_ref), (grad_ref, gain_out) = refs[:3], refs[3:7], refs[-2:]
        raw, row = mine_ref[...], row_ref[:1, :]
        for got in gots:
            raw = raw + got[: OWN + 8, :].astype(F32)[:OWN]
            row = row + ride_sum(got[OWN + 8 :, :])
        gain = gain_ref[...].astype(F32).reshape(1, D)
        gain_out[...] = fold(row / gain)
        w = w_ref[:OWN, :1]
        floats = x_ref[...].astype(F32)
        inv_rms = lax.rsqrt(jnp.mean(floats * floats, axis=-1, keepdims=True) + 1e-06)
        normed = floats * inv_rms
        dn = raw * w * gain
        inner = jnp.mean(dn * normed, axis=-1, keepdims=True)
        ge = (cot_ref[...].astype(F32) * w).astype(BF16).astype(F32)
        grad_ref[...] = (ge + inv_rms * (dn - normed * inner)).astype(BF16)

    return pl.pallas_call(
        kernel,
        in_specs=here(9) + [pl.BlockSpec(memory_space=pl.ANY)] * len(first),
        out_specs=tuple(here(2)),
        out_shape=(shape(OWN, D), shape(8, 128, dtype=F32)),
        compiler_params=params(4),
        cost_estimate=cost(MIB, MIB),
        name="raw_last",
    )(mine, row, *gots, weight, inputs, cotangent, gain, *first)


def body(inputs, cotangent, segment_ids, norm_gain, w_in, w_out):
    dp = lax.axis_index("dp")
    y_lo, z = lax.div(dp, 8), lax.rem(dp, 8)
    spot = jnp.stack([y_lo, z])
    packed = pack(spot, inputs, cotangent, segment_ids, norm_gain)

    row = jnp.concatenate([packed] + [send(packed, first_axis(-o)) for o in OFFSETS[1:]], axis=0)
    w_in = lax.dynamic_slice_in_dim(w_in, y_lo * HID, HID, 1)
    w_out = lax.dynamic_slice_in_dim(w_out, y_lo * HID, HID, 0)
    plus, minus = send(row, second_axis(-1)), send(row, second_axis(1))
    swapped = send(copied(row, w_in, w_out), other_core)
    parts = [chunk(0, [row, swapped], w_in, w_out)]
    plus, minus = after([plus, minus], parts[0][1])
    relayed = [
        send(part, second_axis(o)) for part, o in zip(relay_halves(plus, minus), (-1, 1))
    ]
    parts.append(chunk(1, [plus, send(plus, other_core)], w_in, w_out))
    swapped = send(minus, other_core)
    parts.append(chunk(2, [minus, swapped], w_in, w_out, parts[1][1]))
    relayed = after(relayed, parts[2][1])
    parts.append(chunk(3, [*relayed, *(send(r, other_core) for r in relayed)], w_in, w_out))
    lefts, labs, rights, mine, theirs = zip(*parts)

    weight, up, down, theirs_all = far_call(spot, labs, lefts, rights, theirs)
    up_got, down_got = send(up, along_z(1)), send(down, along_z(-1))
    raw_got = send(theirs_all, other_core)
    raws = [raw for pair in zip(mine, theirs) for raw in pair]
    gain = gain_call(weight, lefts, raws)
    gain_got = send(gain, other_core)
    near = terms_call("near_terms", [(3, -3)], spot, weight, lefts, rights, gain)
    gain = gain + gain_got
    gain = gain + send(gain, xor_z(1))
    keep, *blocks = raw_first(mine, raw_got, gain, near)
    gots = [send(blocks[j], second_axis(OFFSETS[j + 1])) for j in (2, 0, 1)]

    up, down = ring_call(1, 0, near, up_got, down_got, *blocks)
    up_got, down_got = send(up, along_z(1)), send(down, along_z(-1))
    middle = terms_call("middle_terms", [(2, -2)], spot, weight, lefts, rights, up)

    up, down = ring_call(2, 0, middle, up_got, down_got, *gots)
    up_got, down_got = send(up, along_z(1)), send(down, along_z(-1))
    rest = terms_call("rest_terms", [(1, -1), (0,)], spot, weight, lefts, rights, up)
    own, row_sum, *blocks = raw_second(keep, gain, gots, up, down)
    gots = [send(blocks[j], first_axis(OFFSETS[j + 1])) for j in (2, 0, 1)]

    up, down = ring_call(3, 0, rest, up_got, down_got, *gots)
    up_got, down_got = send(up, along_z(1)), send(down, along_z(-1))
    input_grad, gain_grad = raw_last(
        own, row_sum, gots, weight, inputs, cotangent, norm_gain, up, down
    )
    gain_grad = gain_grad + sum(send(gain_grad, xor_z(o)) for o in (2, 4, 6))

    sums, give = ring_last(spot, 2, rest, up_got, down_got, gain_grad)
    outs = place(0, spot, sums, give)
    w_out_grad, w_in_grad = place(1, spot, send(give, partner_y), *outs)
    return (input_grad, w_in_grad, w_out_grad.T, gain_grad.reshape(D))


def solution(mesh):
    in_specs = (
        P(("dp", "mp"), None),
        P(("dp", "mp"), None),
        P("dp", "mp"),
        P(),
        P(None, "mp"),
        P("mp", None),
    )
    out_specs = (P(("dp", "mp"), None), P("dp", "mp"), P("mp", "dp"), P())
    return jax.shard_map(body, mesh=mesh, in_specs=in_specs, out_specs=out_specs, check_vma=False)
```

```python
import functools
import math

import jax
import jax.numpy as jnp
from jax import lax
from jax.experimental import pallas as pl
from jax.experimental.pallas import tpu as pltpu
from jax.sharding import PartitionSpec as P

TOK_GROUP = 640
SEGS = 8
OWN = 40
ROW = 4 * OWN
CHUNK = 2 * ROW
PLANE = 4 * CHUNK
D = 1024
HID = 1024
PACK = 2 * D + 128
AXES = ("dp", "mp")
OFFSETS = (0, 1, -1, 2)
MIB = 1024 * 1024

GELU_C = 0.7978845608
GELU_A = 0.044715
F32, BF16 = jnp.float32, jnp.bfloat16


def coords(index):
    dp, mp = divmod(index, 16)
    return ((mp // 2) % 4, (mp // 8) * 2 + dp // 8, dp % 8, mp % 2)


def index_of(x, y, z, c):
    x, y, z = x % 4, y % 4, z % 8
    return ((y % 2) * 8 + z) * 16 + ((y // 2) * 4 + x) * 2 + c


def send(value, move):
    pairs = [(i, index_of(*move(*coords(i)))) for i in range(256)]
    return lax.ppermute(value, AXES, pairs)


def first_axis(o):
    return lambda x, y, z, c: (x + o, y, z, c) if c == 0 else (x, y + o, z, c)


def second_axis(o):
    return lambda x, y, z, c: (x, y + o, z, c) if c == 0 else (x + o, y, z, c)


def other_core(x, y, z, c):
    return (x, y, z, 1 - c)


def partner_y(x, y, z, c):
    return (x, y ^ 1, z, c)


def along_z(o):
    return lambda x, y, z, c: (x, y, z + o, c)


def xor_z(o):
    return lambda x, y, z, c: (x, y, z ^ o, c)


def params(mib):
    return pltpu.CompilerParams(vmem_limit_bytes=mib * MIB)


def cost(flops, moved, trans=0):
    return pl.CostEstimate(flops=flops, bytes_accessed=moved, transcendentals=trans)


def here(count):
    return [pl.BlockSpec(memory_space=pltpu.VMEM)] * count


def scalar():
    return pl.BlockSpec(memory_space=pltpu.SMEM)


def shape(*dims, dtype=BF16):
    return jax.ShapeDtypeStruct(dims, dtype)


def pack_kernel(spot_ref, x_hbm, cot_hbm, ids_hbm, gain_hbm, out_ref, x_ref, cot_ref, ids_ref, gain_ref, sems):
    copies = [
        pltpu.make_async_copy(src, dst, sems.at[k])
        for k, (src, dst) in enumerate(
            [(x_hbm, x_ref), (cot_hbm, cot_ref), (ids_hbm, ids_ref), (gain_hbm, gain_ref)]
        )
    ]
    for copy in copies:
        copy.start()
    for copy in copies:
        copy.wait()
    floats = x_ref[...].astype(F32)
    inv_rms = lax.rsqrt(jnp.mean(floats * floats, axis=-1, keepdims=True) + 1e-06)
    normed = floats * inv_rms
    out_ref[:, :D] = cot_ref[...]
    out_ref[:, D : 2 * D] = (normed * gain_ref[...].astype(F32).reshape(1, D)).astype(BF16)
    ids = jnp.broadcast_to((ids_ref[...] + SEGS * spot_ref[0]).astype(F32), (OWN, OWN))
    along = lax.broadcasted_iota(jnp.int32, (OWN, OWN), 0)
    across = lax.broadcasted_iota(jnp.int32, (OWN, OWN), 1)
    label = jnp.sum(jnp.where(along == across, ids, 0.0), axis=1, keepdims=True)
    out_ref[:, 2 * D :] = jnp.broadcast_to(label, (OWN, 128)).astype(BF16)


def pack(spot, inputs, cotangent, ids, gain):
    inputs_in_hbm = [
        pltpu.with_memory_space_constraint(a, pltpu.HBM) for a in (inputs, cotangent, ids, gain)
    ]
    return pl.pallas_call(
        pack_kernel,
        in_specs=[pl.BlockSpec(memory_space=pltpu.SMEM)]
        + [pl.BlockSpec(memory_space=pltpu.HBM)] * 4,
        out_shape=jax.ShapeDtypeStruct((OWN, PACK), BF16),
        scratch_shapes=[
            pltpu.VMEM((OWN, D), BF16),
            pltpu.VMEM((OWN, D), BF16),
            pltpu.VMEM((1, OWN), jnp.int32),
            pltpu.VMEM((D,), BF16),
            pltpu.SemaphoreType.DMA((4,)),
        ],
        compiler_params=params(4),
        cost_estimate=cost(OWN * D * 8, 4 * OWN * D * 2),
        name="pack_rows",
    )(spot, *inputs_in_hbm)


def nothing(*refs):
    pass


def after(values, *first):
    anywhere = pl.BlockSpec(memory_space=pl.ANY)
    return pl.pallas_call(
        nothing,
        in_specs=[anywhere] * (len(values) + len(first)),
        out_specs=[anywhere] * len(values),
        out_shape=[jax.ShapeDtypeStruct(v.shape, v.dtype) for v in values],
        input_output_aliases={k: k for k in range(len(values))},
        compiler_params=params(1),
        cost_estimate=cost(0, 0),
        name="after",
    )(*values, *first)


def copied(value, *first):
    def kernel(value_ref, *refs):
        refs[-1][...] = value_ref[...]

    return pl.pallas_call(
        kernel,
        in_specs=here(1) + [pl.BlockSpec(memory_space=pl.ANY)] * len(first),
        out_specs=here(1)[0],
        out_shape=shape(*value.shape),
        compiler_params=params(2),
        cost_estimate=cost(0, MIB),
        name="copied",
    )(value, *first)


def relay_halves(plus, minus, *first):
    def kernel(plus_ref, minus_ref, *refs):
        refs[-2][...] = plus_ref[: ROW // 2, :]
        refs[-1][...] = minus_ref[ROW // 2 :, :]

    return pl.pallas_call(
        kernel,
        in_specs=here(2) + [pl.BlockSpec(memory_space=pl.ANY)] * len(first),
        out_specs=tuple(here(2)),
        out_shape=(shape(ROW // 2, PACK),) * 2,
        compiler_params=params(2),
        cost_estimate=cost(0, MIB),
        name="relay_halves",
    )(plus, minus, *first)


STEPS = 1
WIDTH = HID // STEPS


def chunk_kernel(count, *refs):
    srcs, (w_in_ref, w_out_ref) = refs[:count], refs[count : count + 2]
    left_ref, lab_ref, right_ref, mine_ref, theirs_ref, acc = refs[-6:]
    size = CHUNK // count
    for k, src in enumerate(srcs):
        rows = slice(k * size, (k + 1) * size)
        left_ref[rows, :] = src[:, : 2 * D]
        lab_ref[rows, :] = src[:, 2 * D :]
    for step in range(STEPS):
        cols = slice(step * WIDTH, (step + 1) * WIDTH)
        p = jnp.dot(left_ref[:, D:], w_in_ref[:, cols], preferred_element_type=F32)
        g = lax.dot_general(
            left_ref[:, :D], w_out_ref[cols, :], (((1,), (1,)), ((), ())), preferred_element_type=F32
        )
        p2 = p * p
        h = 0.5 * jnp.tanh(p * (GELU_C + (GELU_C * GELU_A) * p2)) + 0.5
        q = p * (2.0 * GELU_C + (6.0 * GELU_C * GELU_A) * p2)
        right_ref[:, cols] = (p * h).astype(BF16)
        pre_grad = (g * (h * (1.0 + (q - q * h)))).astype(BF16)
        right_ref[:, HID + step * WIDTH : HID + (step + 1) * WIDTH] = pre_grad
        raw = lax.dot_general(
            pre_grad, w_in_ref[:, cols], (((1,), (1,)), ((), ())), preferred_element_type=F32
        )
        if step > 0:
            raw = raw + acc[...]
        if step < STEPS - 1:
            acc[...] = raw
        else:
            mine_ref[...] = raw[:ROW].astype(BF16)
            theirs_ref[...] = raw[ROW:].astype(BF16)


def chunk(j, srcs, w_in, w_out, *first):
    shapes = [(CHUNK, 2 * D), (CHUNK, 128), (CHUNK, 2 * HID), (ROW, D), (ROW, D)]
    return pl.pallas_call(
        functools.partial(chunk_kernel, len(srcs)),
        in_specs=here(len(srcs) + 2) + [pl.BlockSpec(memory_space=pl.ANY)] * len(first),
        out_specs=here(5),
        scratch_shapes=[pltpu.VMEM((CHUNK, D), F32)],
        out_shape=[shape(*s) for s in shapes],
        compiler_params=params(14),
        cost_estimate=cost(*((10**8, MIB) if j == 0 else (6 * CHUNK * D * HID, 9 * MIB, CHUNK * HID))),
        name="chunk_%d" % j,
    )(*srcs, w_in, w_out, *first)


def token_weights(labels):
    labels = labels.astype(F32)
    lanes = lax.broadcasted_iota(jnp.int32, (PLANE, 128), 1).astype(F32)
    onehot = jnp.where(labels == lanes, 1.0, 0.0)
    counts = jnp.sum(onehot, axis=0, keepdims=True)
    token_count = jnp.sum(onehot * counts, axis=1, keepdims=True)
    weights = jnp.sqrt(TOK_GROUP / (SEGS * token_count))
    padding = jnp.sum(onehot * jnp.where((lanes == 7.0) | (lanes == 15.0), 1.0, 0.0), axis=1, keepdims=True)
    return jnp.where(padding > 0.5, 0.0, weights)


GRAD_SCALE = 1.0 / math.sqrt(TOK_GROUP * 16)


RIDE = 16


def fold(row):
    return jnp.concatenate([row[:, k * 128 : (k + 1) * 128] for k in range(8)], axis=0)


def unfold(block):
    return jnp.concatenate([block[k : k + 1, :] for k in range(8)], axis=1)


def gain_call(weight, lefts, raws, *first):
    def kernel(w_ref, *refs):
        lefts, raws, gain_ref = refs[:4], refs[4:12], refs[-1]
        total = jnp.zeros((1, D), F32)
        for k, raw in enumerate(raws):
            rows = slice((k % 2) * ROW, (k % 2 + 1) * ROW)
            w = w_ref[k * ROW : (k + 1) * ROW, :1]
            term = lefts[k // 2][rows, D:].astype(F32) * raw[...].astype(F32) * w
            total = total + jnp.sum(term, axis=0, keepdims=True)
        gain_ref[...] = fold(total)

    anywhere = pl.BlockSpec(memory_space=pl.ANY)
    return pl.pallas_call(
        kernel,
        in_specs=here(13) + [anywhere] * len(first),
        out_shape=shape(8, 128, dtype=F32),
        compiler_params=params(8),
        cost_estimate=cost(4 * PLANE * D, 8 * MIB),
        name="gain_term",
    )(weight, *lefts, *raws, *first)


def term_block(array, offsets, z, weight, lefts, rights):
    low = (lax.broadcasted_iota(jnp.int32, (PLANE, 128), 1) < 64).astype(jnp.int32)
    blocks = []
    for offset in offsets:
        to = lax.rem(z + offset + 8, 8)
        odd = lax.rem(to, 2)
        start = array * D + (to // 2) * 128
        moved, kept = (
            jnp.concatenate([ref[:, pl.ds(pl.multiple_of(at, 128), 128)] for ref in lefts], axis=0)
            for at in (start + (1 - odd) * (D // 2), start + odd * (D // 2))
        )
        moved = pltpu.roll(moved.astype(F32), 64, 1)
        blocks.append((jnp.where(low == odd, moved, kept.astype(F32)) * weight).astype(BF16))
    left = jnp.concatenate(blocks, axis=1)
    right = jnp.concatenate([ref[:, array * HID : (array + 1) * HID] for ref in rights], axis=0)
    total = lax.dot_general(left, right, (((0,), (0,)), ((), ())), preferred_element_type=F32)
    return (total * GRAD_SCALE).astype(BF16)


def far_call(spot, labs, lefts, rights, theirs):
    def kernel(spot_ref, *refs):
        labs, lefts, rights, theirs = refs[:4], refs[4:8], refs[8:12], refs[12:16]
        weight_ref, up_ref, down_ref, theirs_ref = refs[16:]
        weights = token_weights(jnp.concatenate([lab[...] for lab in labs], axis=0))
        weight_ref[...] = jnp.broadcast_to(weights, (PLANE, 128))
        for array, ref in enumerate((up_ref, down_ref)):
            block = term_block(array, (4,), spot_ref[1], weight_ref[...], lefts, rights)
            ref[...] = block.reshape(2, 64, HID)
        for j, raw in enumerate(theirs):
            theirs_ref[j * ROW : (j + 1) * ROW, :] = raw[...]

    return pl.pallas_call(
        kernel,
        in_specs=[scalar()] + here(16),
        out_specs=tuple(here(4)),
        out_shape=(
            shape(PLANE, 128, dtype=F32),
            shape(2, 64, HID),
            shape(2, 64, HID),
            shape(TOK_GROUP, D),
        ),
        compiler_params=params(12),
        cost_estimate=cost(PLANE * D * HID, 8 * MIB),
        name="far_terms",
    )(spot, *labs, *lefts, *rights, *theirs)


def terms_call(name, groups, spot, weight, lefts, rights, *first):
    count = sum(len(group) for group in groups)

    def kernel(spot_ref, weight_ref, *refs):
        lefts, rights, out_ref = refs[:4], refs[4:8], refs[-1]
        at = 0
        for group in groups:
            for array in range(2):
                block = term_block(array, group, spot_ref[1], weight_ref[...], lefts, rights)
                block = block.reshape(len(group), 2, 64, HID)
                for k in range(len(group)):
                    out_ref[at + k, array] = block[k]
            at += len(group)

    return pl.pallas_call(
        kernel,
        in_specs=[scalar()] + here(9) + [pl.BlockSpec(memory_space=pl.ANY)] * len(first),
        out_specs=here(1)[0],
        out_shape=shape(count, 2, 2, 64, HID),
        compiler_params=params(12),
        cost_estimate=cost(count * PLANE * 512 * HID, 8 * MIB),
        name=name,
    )(spot, weight, *lefts, *rights, *first)


def add(*terms):
    return sum(t.astype(F32) for t in terms).astype(BF16)


def ring_call(step, at, terms, plus, minus, *first):
    def kernel(terms_ref, plus_ref, minus_ref, *refs):
        up_ref, down_ref = refs[-2:]
        if step == 1:
            up_ref[0] = add(plus_ref[...], terms_ref[at, 0])
            up_ref[1] = terms_ref[at, 1]
            down_ref[0] = terms_ref[at + 1, 0]
            down_ref[1] = add(minus_ref[...], terms_ref[at + 1, 1])
        else:
            for array in range(2):
                up_ref[array] = add(plus_ref[array], terms_ref[at, array])
                down_ref[array] = add(minus_ref[array], terms_ref[at + 1, array])

    anywhere = pl.BlockSpec(memory_space=pl.ANY)
    return pl.pallas_call(
        kernel,
        in_specs=here(3) + [anywhere] * len(first),
        out_specs=tuple(here(2)),
        out_shape=(shape(2, 2, 64, HID),) * 2,
        compiler_params=params(4),
        cost_estimate=cost(4 * MIB, 4 * MIB),
        name="ring_%d" % step,
    )(terms, plus, minus, *first)


def ring_last(spot, at, terms, plus, minus, *first):
    def kernel(spot_ref, terms_ref, plus_ref, minus_ref, *refs):
        mine_ref, give_ref = refs[-2:]
        own = spot_ref[0]
        for array in range(2):
            for ref, y in ((give_ref, 1 - own), (mine_ref, own)):
                ref[array] = add(terms_ref[at, array, y], plus_ref[array, y], minus_ref[array, y])

    anywhere = pl.BlockSpec(memory_space=pl.ANY)
    return pl.pallas_call(
        kernel,
        in_specs=[scalar()] + here(3) + [anywhere] * len(first),
        out_specs=tuple(here(2)),
        out_shape=(shape(2, 64, HID),) * 2,
        compiler_params=params(4),
        cost_estimate=cost(MIB, 2 * MIB),
        name="ring_last",
    )(spot, terms, plus, minus, *first)


def place(other, spot, half, *outs):
    olds = outs if other else ()

    def kernel(spot_ref, half_ref, *refs):
        *_, first, second, sems = refs
        column = spot_ref[0] if other == 0 else 1 - spot_ref[0]
        cols = pl.ds(pl.multiple_of(column * HID, HID), HID)
        copies = [
            pltpu.make_async_copy(half_ref.at[array], out.at[:, cols], sems.at[array])
            for array, out in enumerate((first, second))
        ]
        for copy in copies:
            copy.start()
        for copy in copies:
            copy.wait()

    anywhere = [pl.BlockSpec(memory_space=pl.ANY)]
    return pl.pallas_call(
        kernel,
        in_specs=[scalar()] + here(1) + anywhere * len(outs),
        out_specs=(pl.BlockSpec(memory_space=pltpu.HBM),) * 2,
        out_shape=(pltpu.HBM((64, 2 * HID), BF16),) * 2,
        scratch_shapes=[pltpu.SemaphoreType.DMA((2,))],
        input_output_aliases={2 + k: k for k in range(len(olds))},
        compiler_params=params(4),
        cost_estimate=cost(MIB, MIB),
        name="place_%d" % other,
    )(spot, half, *outs)


def ride_rows(total):
    high = total.astype(BF16).astype(F32)
    rows = lax.broadcasted_iota(jnp.int32, (RIDE, D), 0)
    return jnp.where(rows == 0, high, jnp.where(rows == 1, total - high, 0.0)).astype(BF16)


def ride_sum(rows):
    return jnp.sum(rows.astype(F32), axis=0, keepdims=True)


def raw_first(mine, got, gain, *first):
    def kernel(*refs):
        mines, got_ref, gain_ref = refs[:4], refs[4], refs[5]
        keep_ref, *sends = refs[-4:]
        keep_ref[...] = mines[0][...].astype(F32) + got_ref[:ROW, :].astype(F32)
        ride = ride_rows(unfold(gain_ref[...]))
        for j in range(1, 4):
            sends[j - 1][:ROW, :] = add(mines[j][...], got_ref[j * ROW : (j + 1) * ROW, :])
            sends[j - 1][ROW:, :] = ride

    anywhere = pl.BlockSpec(memory_space=pl.ANY)
    return pl.pallas_call(
        kernel,
        in_specs=here(6) + [anywhere] * len(first),
        out_specs=tuple(here(4)),
        out_shape=(shape(ROW, D, dtype=F32),) + (shape(ROW + RIDE, D),) * 3,
        compiler_params=params(4),
        cost_estimate=cost(2 * MIB, 4 * MIB),
        name="raw_first",
    )(*mine, got, gain, *first)


def raw_second(keep, gain, gots, *first):
    def kernel(keep_ref, gain_ref, *refs):
        gots = refs[:3]
        mine_ref, total_ref, *sends = refs[-5:]
        total = keep_ref[...]
        row = ride_sum(ride_rows(unfold(gain_ref[...])))
        for got in gots:
            total = total + got[:ROW, :].astype(F32)
            row = row + ride_sum(got[ROW:, :])
        ride = ride_rows(row)
        mine_ref[...] = total[:OWN]
        total_ref[...] = jnp.broadcast_to(ride_sum(ride), (8, D))
        for j in range(1, 4):
            block = jnp.concatenate([total[j * OWN : (j + 1) * OWN], jnp.zeros((8, D), F32)], axis=0)
            sends[j - 1][: OWN + 8, :] = block.astype(BF16)
            sends[j - 1][OWN + 8 :, :] = ride

    anywhere = pl.BlockSpec(memory_space=pl.ANY)
    return pl.pallas_call(
        kernel,
        in_specs=here(5) + [anywhere] * len(first),
        out_specs=tuple(here(5)),
        out_shape=(shape(OWN, D, dtype=F32), shape(8, D, dtype=F32))
        + (shape(OWN + 8 + RIDE, D),) * 3,
        compiler_params=params(6),
        cost_estimate=cost(2 * MIB, 2 * MIB),
        name="raw_second",
    )(keep, gain, *gots, *first)


def raw_last(mine, row, gots, weight, inputs, cotangent, gain, *first):
    def kernel(mine_ref, row_ref, *refs):
        gots, (w_ref, x_ref, cot_ref, gain_ref), (grad_ref, gain_out) = refs[:3], refs[3:7], refs[-2:]
        raw, row = mine_ref[...], row_ref[:1, :]
        for got in gots:
            raw = raw + got[: OWN + 8, :].astype(F32)[:OWN]
            row = row + ride_sum(got[OWN + 8 :, :])
        gain = gain_ref[...].astype(F32).reshape(1, D)
        gain_out[...] = fold(row / gain)
        w = w_ref[:OWN, :1]
        floats = x_ref[...].astype(F32)
        inv_rms = lax.rsqrt(jnp.mean(floats * floats, axis=-1, keepdims=True) + 1e-06)
        normed = floats * inv_rms
        dn = raw * w * gain
        inner = jnp.mean(dn * normed, axis=-1, keepdims=True)
        ge = (cot_ref[...].astype(F32) * w).astype(BF16).astype(F32)
        grad_ref[...] = (ge + inv_rms * (dn - normed * inner)).astype(BF16)

    return pl.pallas_call(
        kernel,
        in_specs=here(9) + [pl.BlockSpec(memory_space=pl.ANY)] * len(first),
        out_specs=tuple(here(2)),
        out_shape=(shape(OWN, D), shape(8, 128, dtype=F32)),
        compiler_params=params(4),
        cost_estimate=cost(MIB, MIB),
        name="raw_last",
    )(mine, row, *gots, weight, inputs, cotangent, gain, *first)


def body(inputs, cotangent, segment_ids, norm_gain, w_in, w_out):
    dp = lax.axis_index("dp")
    y_lo, z = lax.div(dp, 8), lax.rem(dp, 8)
    spot = jnp.stack([y_lo, z])
    packed = pack(spot, inputs, cotangent, segment_ids, norm_gain)

    row = jnp.concatenate([packed] + [send(packed, first_axis(-o)) for o in OFFSETS[1:]], axis=0)
    w_in = lax.dynamic_slice_in_dim(w_in, y_lo * HID, HID, 1)
    w_out = lax.dynamic_slice_in_dim(w_out, y_lo * HID, HID, 0)
    plus, minus = send(row, second_axis(-1)), send(row, second_axis(1))
    swapped = send(copied(row, w_in, w_out), other_core)
    parts = [chunk(0, [row, swapped], w_in, w_out)]
    plus, minus = after([plus, minus], parts[0][1])
    relayed = [
        send(part, second_axis(o)) for part, o in zip(relay_halves(plus, minus), (-1, 1))
    ]
    parts.append(chunk(1, [plus, send(plus, other_core)], w_in, w_out))
    swapped = send(minus, other_core)
    parts.append(chunk(2, [minus, swapped], w_in, w_out, parts[1][1]))
    relayed = after(relayed, parts[2][1])
    parts.append(chunk(3, [*relayed, *(send(r, other_core) for r in relayed)], w_in, w_out))
    lefts, labs, rights, mine, theirs = zip(*parts)

    weight, up, down, theirs_all = far_call(spot, labs, lefts, rights, theirs)
    up_got, down_got = send(up, along_z(1)), send(down, along_z(-1))
    raw_got = send(theirs_all, other_core)
    raws = [raw for pair in zip(mine, theirs) for raw in pair]
    gain = gain_call(weight, lefts, raws)
    gain_got = send(gain, other_core)
    near = terms_call("near_terms", [(3, -3)], spot, weight, lefts, rights, gain)
    gain = gain + gain_got
    gain = gain + send(gain, xor_z(1))
    keep, *blocks = raw_first(mine, raw_got, gain, near)
    gots = [send(blocks[j], second_axis(OFFSETS[j + 1])) for j in (2, 0, 1)]

    up, down = ring_call(1, 0, near, up_got, down_got, *blocks)
    up_got, down_got = send(up, along_z(1)), send(down, along_z(-1))
    middle = terms_call("middle_terms", [(2, -2)], spot, weight, lefts, rights, up)

    up, down = ring_call(2, 0, middle, up_got, down_got, *gots)
    up_got, down_got = send(up, along_z(1)), send(down, along_z(-1))
    rest = terms_call("rest_terms", [(1, -1), (0,)], spot, weight, lefts, rights, up)
    own, row_sum, *blocks = raw_second(keep, gain, gots, up, down)
    gots = [send(blocks[j], first_axis(OFFSETS[j + 1])) for j in (2, 0, 1)]

    up, down = ring_call(3, 0, rest, up_got, down_got, *gots)
    up_got, down_got = send(up, along_z(1)), send(down, along_z(-1))
    input_grad, gain_grad = raw_last(
        own, row_sum, gots, weight, inputs, cotangent, norm_gain, up, down
    )
    gain_grad = gain_grad + sum(send(gain_grad, xor_z(o)) for o in (2, 4, 6))

    sums, give = ring_last(spot, 2, rest, up_got, down_got, gain_grad)
    outs = place(0, spot, sums, give)
    w_out_grad, w_in_grad = place(1, spot, send(give, partner_y), *outs)
    return (input_grad, w_in_grad, w_out_grad.T, gain_grad.reshape(D))


def solution(mesh):
    in_specs = (
        P(("dp", "mp"), None),
        P(("dp", "mp"), None),
        P("dp", "mp"),
        P(),
        P(None, "mp"),
        P("mp", None),
    )
    out_specs = (P(("dp", "mp"), None), P("dp", "mp"), P("mp", "dp"), P())
    return jax.shard_map(body, mesh=mesh, in_specs=in_specs, out_specs=out_specs, check_vma=False)
```

```python
import functools
import math

import jax
import jax.numpy as jnp
from jax import lax
from jax.experimental import pallas as pl
from jax.experimental.pallas import tpu as pltpu
from jax.sharding import PartitionSpec as P

TOK_GROUP = 640
SEGS = 8
OWN = 40
ROW = 4 * OWN
CHUNK = 2 * ROW
PLANE = 4 * CHUNK
D = 1024
HID = 1024
PACK = 2 * D + 128
AXES = ("dp", "mp")
OFFSETS = (0, 1, -1, 2)
MIB = 1024 * 1024

GELU_C = 0.7978845608
GELU_A = 0.044715
F32, BF16 = jnp.float32, jnp.bfloat16


def coords(index):
    dp, mp = divmod(index, 16)
    return ((mp // 2) % 4, (mp // 8) * 2 + dp // 8, dp % 8, mp % 2)


def index_of(x, y, z, c):
    x, y, z = x % 4, y % 4, z % 8
    return ((y % 2) * 8 + z) * 16 + ((y // 2) * 4 + x) * 2 + c


def send(value, move):
    pairs = [(i, index_of(*move(*coords(i)))) for i in range(256)]
    return lax.ppermute(value, AXES, pairs)


def first_axis(o):
    return lambda x, y, z, c: (x + o, y, z, c) if c == 0 else (x, y + o, z, c)


def second_axis(o):
    return lambda x, y, z, c: (x, y + o, z, c) if c == 0 else (x + o, y, z, c)


def other_core(x, y, z, c):
    return (x, y, z, 1 - c)


def partner_y(x, y, z, c):
    return (x, y ^ 1, z, c)


def along_z(o):
    return lambda x, y, z, c: (x, y, z + o, c)


def xor_z(o):
    return lambda x, y, z, c: (x, y, z ^ o, c)


def params(mib):
    return pltpu.CompilerParams(vmem_limit_bytes=mib * MIB)


def cost(flops, moved, trans=0):
    return pl.CostEstimate(flops=flops, bytes_accessed=moved, transcendentals=trans)


def here(count):
    return [pl.BlockSpec(memory_space=pltpu.VMEM)] * count


def scalar():
    return pl.BlockSpec(memory_space=pltpu.SMEM)


def shape(*dims, dtype=BF16):
    return jax.ShapeDtypeStruct(dims, dtype)


def pack_kernel(spot_ref, x_hbm, cot_hbm, ids_hbm, gain_hbm, out_ref, x_ref, cot_ref, ids_ref, gain_ref, sems):
    copies = [
        pltpu.make_async_copy(src, dst, sems.at[k])
        for k, (src, dst) in enumerate(
            [(x_hbm, x_ref), (cot_hbm, cot_ref), (ids_hbm, ids_ref), (gain_hbm, gain_ref)]
        )
    ]
    for copy in copies:
        copy.start()
    for copy in copies:
        copy.wait()
    floats = x_ref[...].astype(F32)
    inv_rms = lax.rsqrt(jnp.mean(floats * floats, axis=-1, keepdims=True) + 1e-06)
    normed = floats * inv_rms
    out_ref[:, :D] = cot_ref[...]
    out_ref[:, D : 2 * D] = (normed * gain_ref[...].astype(F32).reshape(1, D)).astype(BF16)
    ids = jnp.broadcast_to((ids_ref[...] + SEGS * spot_ref[0]).astype(F32), (OWN, OWN))
    along = lax.broadcasted_iota(jnp.int32, (OWN, OWN), 0)
    across = lax.broadcasted_iota(jnp.int32, (OWN, OWN), 1)
    label = jnp.sum(jnp.where(along == across, ids, 0.0), axis=1, keepdims=True)
    out_ref[:, 2 * D :] = jnp.broadcast_to(label, (OWN, 128)).astype(BF16)


def pack(spot, inputs, cotangent, ids, gain):
    inputs_in_hbm = [
        pltpu.with_memory_space_constraint(a, pltpu.HBM) for a in (inputs, cotangent, ids, gain)
    ]
    return pl.pallas_call(
        pack_kernel,
        in_specs=[pl.BlockSpec(memory_space=pltpu.SMEM)]
        + [pl.BlockSpec(memory_space=pltpu.HBM)] * 4,
        out_shape=jax.ShapeDtypeStruct((OWN, PACK), BF16),
        scratch_shapes=[
            pltpu.VMEM((OWN, D), BF16),
            pltpu.VMEM((OWN, D), BF16),
            pltpu.VMEM((1, OWN), jnp.int32),
            pltpu.VMEM((D,), BF16),
            pltpu.SemaphoreType.DMA((4,)),
        ],
        compiler_params=params(4),
        cost_estimate=cost(OWN * D * 8, 4 * OWN * D * 2),
        name="pack_rows",
    )(spot, *inputs_in_hbm)


def nothing(*refs):
    pass


def after(values, *first):
    anywhere = pl.BlockSpec(memory_space=pl.ANY)
    return pl.pallas_call(
        nothing,
        in_specs=[anywhere] * (len(values) + len(first)),
        out_specs=[anywhere] * len(values),
        out_shape=[jax.ShapeDtypeStruct(v.shape, v.dtype) for v in values],
        input_output_aliases={k: k for k in range(len(values))},
        compiler_params=params(1),
        cost_estimate=cost(0, 0),
        name="after",
    )(*values, *first)


def copied(value, *first):
    def kernel(value_ref, *refs):
        refs[-1][...] = value_ref[...]

    return pl.pallas_call(
        kernel,
        in_specs=here(1) + [pl.BlockSpec(memory_space=pl.ANY)] * len(first),
        out_specs=here(1)[0],
        out_shape=shape(*value.shape),
        compiler_params=params(2),
        cost_estimate=cost(0, MIB),
        name="copied",
    )(value, *first)


def relay_halves(plus, minus, *first):
    def kernel(plus_ref, minus_ref, *refs):
        refs[-2][...] = plus_ref[: ROW // 2, :]
        refs[-1][...] = minus_ref[ROW // 2 :, :]

    return pl.pallas_call(
        kernel,
        in_specs=here(2) + [pl.BlockSpec(memory_space=pl.ANY)] * len(first),
        out_specs=tuple(here(2)),
        out_shape=(shape(ROW // 2, PACK),) * 2,
        compiler_params=params(2),
        cost_estimate=cost(0, MIB),
        name="relay_halves",
    )(plus, minus, *first)


STEPS = 1
WIDTH = HID // STEPS


def chunk_kernel(count, *refs):
    srcs, (w_in_ref, w_out_ref) = refs[:count], refs[count : count + 2]
    left_ref, lab_ref, right_ref, mine_ref, theirs_ref, acc = refs[-6:]
    size = CHUNK // count
    for k, src in enumerate(srcs):
        rows = slice(k * size, (k + 1) * size)
        left_ref[rows, :] = src[:, : 2 * D]
        lab_ref[rows, :] = src[:, 2 * D :]
    for step in range(STEPS):
        cols = slice(step * WIDTH, (step + 1) * WIDTH)
        p = jnp.dot(left_ref[:, D:], w_in_ref[:, cols], preferred_element_type=F32)
        g = lax.dot_general(
            left_ref[:, :D], w_out_ref[cols, :], (((1,), (1,)), ((), ())), preferred_element_type=F32
        )
        p2 = p * p
        h = 0.5 * jnp.tanh(p * (GELU_C + (GELU_C * GELU_A) * p2)) + 0.5
        q = p * (2.0 * GELU_C + (6.0 * GELU_C * GELU_A) * p2)
        right_ref[:, cols] = (p * h).astype(BF16)
        pre_grad = (g * (h * (1.0 + (q - q * h)))).astype(BF16)
        right_ref[:, HID + step * WIDTH : HID + (step + 1) * WIDTH] = pre_grad
        raw = lax.dot_general(
            pre_grad, w_in_ref[:, cols], (((1,), (1,)), ((), ())), preferred_element_type=F32
        )
        if step > 0:
            raw = raw + acc[...]
        if step < STEPS - 1:
            acc[...] = raw
        else:
            mine_ref[...] = raw[:ROW].astype(BF16)
            theirs_ref[...] = raw[ROW:].astype(BF16)


def chunk(j, srcs, w_in, w_out, *first):
    shapes = [(CHUNK, 2 * D), (CHUNK, 128), (CHUNK, 2 * HID), (ROW, D), (ROW, D)]
    return pl.pallas_call(
        functools.partial(chunk_kernel, len(srcs)),
        in_specs=here(len(srcs) + 2) + [pl.BlockSpec(memory_space=pl.ANY)] * len(first),
        out_specs=here(5),
        scratch_shapes=[pltpu.VMEM((CHUNK, D), F32)],
        out_shape=[shape(*s) for s in shapes],
        compiler_params=params(14),
        cost_estimate=cost(*((10**8, MIB) if j == 0 else (6 * CHUNK * D * HID, 9 * MIB, CHUNK * HID))),
        name="chunk_%d" % j,
    )(*srcs, w_in, w_out, *first)


def token_weights(labels):
    labels = labels.astype(F32)
    lanes = lax.broadcasted_iota(jnp.int32, (PLANE, 128), 1).astype(F32)
    onehot = jnp.where(labels == lanes, 1.0, 0.0)
    counts = jnp.sum(onehot, axis=0, keepdims=True)
    lane = lax.broadcasted_iota(jnp.int32, (1, 128), 1)
    none = (lane == SEGS - 1) | (lane == 2 * SEGS - 1) | (counts == 0.0)
    table = jnp.where(none, 0.0, jnp.sqrt(TOK_GROUP / (SEGS * jnp.maximum(counts, 1.0))))
    return jnp.sum(onehot * table, axis=1, keepdims=True)


GRAD_SCALE = 1.0 / math.sqrt(TOK_GROUP * 16)


RIDE = 16


def fold(row):
    return jnp.concatenate([row[:, k * 128 : (k + 1) * 128] for k in range(8)], axis=0)


def unfold(block):
    return jnp.concatenate([block[k : k + 1, :] for k in range(8)], axis=1)


def gain_call(weight, lefts, raws, *first):
    def kernel(w_ref, *refs):
        lefts, raws, gain_ref = refs[:4], refs[4:12], refs[-1]
        total = jnp.zeros((1, D), F32)
        for k, raw in enumerate(raws):
            rows = slice((k % 2) * ROW, (k % 2 + 1) * ROW)
            w = w_ref[k * ROW : (k + 1) * ROW, :1]
            term = lefts[k // 2][rows, D:].astype(F32) * raw[...].astype(F32) * w
            total = total + jnp.sum(term, axis=0, keepdims=True)
        gain_ref[...] = fold(total)

    anywhere = pl.BlockSpec(memory_space=pl.ANY)
    return pl.pallas_call(
        kernel,
        in_specs=here(13) + [anywhere] * len(first),
        out_shape=shape(8, 128, dtype=F32),
        compiler_params=params(8),
        cost_estimate=cost(4 * PLANE * D, 8 * MIB),
        name="gain_term",
    )(weight, *lefts, *raws, *first)


def term_block(array, offsets, z, weight, lefts, rights):
    low = (lax.broadcasted_iota(jnp.int32, (PLANE, 128), 1) < 64).astype(jnp.int32)
    blocks = []
    for offset in offsets:
        to = lax.rem(z + offset + 8, 8)
        odd = lax.rem(to, 2)
        start = array * D + (to // 2) * 128
        moved, kept = (
            jnp.concatenate([ref[:, pl.ds(pl.multiple_of(at, 128), 128)] for ref in lefts], axis=0)
            for at in (start + (1 - odd) * (D // 2), start + odd * (D // 2))
        )
        moved = pltpu.roll(moved.astype(F32), 64, 1)
        blocks.append((jnp.where(low == odd, moved, kept.astype(F32)) * weight).astype(BF16))
    left = jnp.concatenate(blocks, axis=1)
    right = jnp.concatenate([ref[:, array * HID : (array + 1) * HID] for ref in rights], axis=0)
    total = lax.dot_general(left, right, (((0,), (0,)), ((), ())), preferred_element_type=F32)
    return (total * GRAD_SCALE).astype(BF16)


def far_call(spot, labs, lefts, rights, theirs):
    def kernel(spot_ref, *refs):
        labs, lefts, rights, theirs = refs[:4], refs[4:8], refs[8:12], refs[12:16]
        weight_ref, up_ref, down_ref, theirs_ref = refs[16:]
        weights = token_weights(jnp.concatenate([lab[...] for lab in labs], axis=0))
        weight_ref[...] = jnp.broadcast_to(weights, (PLANE, 128))
        for array, ref in enumerate((up_ref, down_ref)):
            block = term_block(array, (4,), spot_ref[1], weight_ref[...], lefts, rights)
            ref[...] = block.reshape(2, 64, HID)
        for j, raw in enumerate(theirs):
            theirs_ref[j * ROW : (j + 1) * ROW, :] = raw[...]

    return pl.pallas_call(
        kernel,
        in_specs=[scalar()] + here(16),
        out_specs=tuple(here(4)),
        out_shape=(
            shape(PLANE, 128, dtype=F32),
            shape(2, 64, HID),
            shape(2, 64, HID),
            shape(TOK_GROUP, D),
        ),
        compiler_params=params(12),
        cost_estimate=cost(PLANE * D * HID, 8 * MIB),
        name="far_terms",
    )(spot, *labs, *lefts, *rights, *theirs)


def terms_call(name, groups, spot, weight, lefts, rights, *first):
    count = sum(len(group) for group in groups)

    def kernel(spot_ref, weight_ref, *refs):
        lefts, rights, out_ref = refs[:4], refs[4:8], refs[-1]
        at = 0
        for group in groups:
            for array in range(2):
                block = term_block(array, group, spot_ref[1], weight_ref[...], lefts, rights)
                block = block.reshape(len(group), 2, 64, HID)
                for k in range(len(group)):
                    out_ref[at + k, array] = block[k]
            at += len(group)

    return pl.pallas_call(
        kernel,
        in_specs=[scalar()] + here(9) + [pl.BlockSpec(memory_space=pl.ANY)] * len(first),
        out_specs=here(1)[0],
        out_shape=shape(count, 2, 2, 64, HID),
        compiler_params=params(12),
        cost_estimate=cost(count * PLANE * 512 * HID, 8 * MIB),
        name=name,
    )(spot, weight, *lefts, *rights, *first)


def add(*terms):
    return sum(t.astype(F32) for t in terms).astype(BF16)


def ring_call(step, at, terms, plus, minus, *first):
    def kernel(terms_ref, plus_ref, minus_ref, *refs):
        up_ref, down_ref = refs[-2:]
        if step == 1:
            up_ref[0] = add(plus_ref[...], terms_ref[at, 0])
            up_ref[1] = terms_ref[at, 1]
            down_ref[0] = terms_ref[at + 1, 0]
            down_ref[1] = add(minus_ref[...], terms_ref[at + 1, 1])
        else:
            for array in range(2):
                up_ref[array] = add(plus_ref[array], terms_ref[at, array])
                down_ref[array] = add(minus_ref[array], terms_ref[at + 1, array])

    anywhere = pl.BlockSpec(memory_space=pl.ANY)
    return pl.pallas_call(
        kernel,
        in_specs=here(3) + [anywhere] * len(first),
        out_specs=tuple(here(2)),
        out_shape=(shape(2, 2, 64, HID),) * 2,
        compiler_params=params(4),
        cost_estimate=cost(4 * MIB, 4 * MIB),
        name="ring_%d" % step,
    )(terms, plus, minus, *first)


def ring_last(other, spot, at, terms, plus, minus, *first):
    def kernel(spot_ref, terms_ref, plus_ref, minus_ref, *refs):
        y = spot_ref[0] if other == 0 else 1 - spot_ref[0]
        for array in range(2):
            refs[-1][array] = add(terms_ref[at, array, y], plus_ref[array, y], minus_ref[array, y])

    anywhere = pl.BlockSpec(memory_space=pl.ANY)
    return pl.pallas_call(
        kernel,
        in_specs=[scalar()] + here(3) + [anywhere] * len(first),
        out_specs=here(1)[0],
        out_shape=shape(2, 64, HID),
        compiler_params=params(4),
        cost_estimate=cost(MIB, 2 * MIB),
        name="ring_last_%d" % other,
    )(spot, terms, plus, minus, *first)


def place(other, spot, half, *outs):
    olds = outs if other else ()

    def kernel(spot_ref, half_ref, *refs):
        *_, first, second, sems = refs
        column = spot_ref[0] if other == 0 else 1 - spot_ref[0]
        cols = pl.ds(pl.multiple_of(column * HID, HID), HID)
        copies = [
            pltpu.make_async_copy(half_ref.at[array], out.at[:, cols], sems.at[array])
            for array, out in enumerate((first, second))
        ]
        for copy in copies:
            copy.start()
        for copy in copies:
            copy.wait()

    anywhere = [pl.BlockSpec(memory_space=pl.ANY)]
    return pl.pallas_call(
        kernel,
        in_specs=[scalar()] + here(1) + anywhere * len(outs),
        out_specs=(pl.BlockSpec(memory_space=pltpu.HBM),) * 2,
        out_shape=(pltpu.HBM((64, 2 * HID), BF16),) * 2,
        scratch_shapes=[pltpu.SemaphoreType.DMA((2,))],
        input_output_aliases={2 + k: k for k in range(len(olds))},
        compiler_params=params(4),
        cost_estimate=cost(MIB, MIB),
        name="place_%d" % other,
    )(spot, half, *outs)


def ride_rows(total):
    high = total.astype(BF16).astype(F32)
    rows = lax.broadcasted_iota(jnp.int32, (RIDE, D), 0)
    return jnp.where(rows == 0, high, jnp.where(rows == 1, total - high, 0.0)).astype(BF16)


def ride_sum(rows):
    return jnp.sum(rows.astype(F32), axis=0, keepdims=True)


def raw_first(mine, got, gain, *first):
    def kernel(*refs):
        mines, got_ref, gain_ref = refs[:4], refs[4], refs[5]
        keep_ref, *sends = refs[-4:]
        keep_ref[...] = mines[0][...].astype(F32) + got_ref[:ROW, :].astype(F32)
        ride = ride_rows(unfold(gain_ref[...]))
        for j in range(1, 4):
            sends[j - 1][:ROW, :] = add(mines[j][...], got_ref[j * ROW : (j + 1) * ROW, :])
            sends[j - 1][ROW:, :] = ride

    anywhere = pl.BlockSpec(memory_space=pl.ANY)
    return pl.pallas_call(
        kernel,
        in_specs=here(6) + [anywhere] * len(first),
        out_specs=tuple(here(4)),
        out_shape=(shape(ROW, D, dtype=F32),) + (shape(ROW + RIDE, D),) * 3,
        compiler_params=params(4),
        cost_estimate=cost(2 * MIB, 4 * MIB),
        name="raw_first",
    )(*mine, got, gain, *first)


def raw_second(keep, gain, gots, *first):
    def kernel(keep_ref, gain_ref, *refs):
        gots = refs[:3]
        mine_ref, total_ref, *sends = refs[-5:]
        total = keep_ref[...]
        row = ride_sum(ride_rows(unfold(gain_ref[...])))
        for got in gots:
            total = total + got[:ROW, :].astype(F32)
            row = row + ride_sum(got[ROW:, :])
        ride = ride_rows(row)
        mine_ref[...] = total[:OWN]
        total_ref[...] = jnp.broadcast_to(ride_sum(ride), (8, D))
        for j in range(1, 4):
            block = jnp.concatenate([total[j * OWN : (j + 1) * OWN], jnp.zeros((8, D), F32)], axis=0)
            sends[j - 1][: OWN + 8, :] = block.astype(BF16)
            sends[j - 1][OWN + 8 :, :] = ride

    anywhere = pl.BlockSpec(memory_space=pl.ANY)
    return pl.pallas_call(
        kernel,
        in_specs=here(5) + [anywhere] * len(first),
        out_specs=tuple(here(5)),
        out_shape=(shape(OWN, D, dtype=F32), shape(8, D, dtype=F32))
        + (shape(OWN + 8 + RIDE, D),) * 3,
        compiler_params=params(6),
        cost_estimate=cost(2 * MIB, 2 * MIB),
        name="raw_second",
    )(keep, gain, *gots, *first)


def raw_last(mine, row, gots, weight, inputs, cotangent, gain, *first):
    def kernel(mine_ref, row_ref, *refs):
        gots, (w_ref, x_ref, cot_ref, gain_ref), (grad_ref, gain_out) = refs[:3], refs[3:7], refs[-2:]
        raw, row = mine_ref[...], row_ref[:1, :]
        for got in gots:
            raw = raw + got[: OWN + 8, :].astype(F32)[:OWN]
            row = row + ride_sum(got[OWN + 8 :, :])
        gain = gain_ref[...].astype(F32).reshape(1, D)
        gain_out[...] = fold(row / gain)
        w = w_ref[:OWN, :1]
        floats = x_ref[...].astype(F32)
        inv_rms = lax.rsqrt(jnp.mean(floats * floats, axis=-1, keepdims=True) + 1e-06)
        normed = floats * inv_rms
        dn = raw * w * gain
        inner = jnp.mean(dn * normed, axis=-1, keepdims=True)
        ge = (cot_ref[...].astype(F32) * w).astype(BF16).astype(F32)
        grad_ref[...] = (ge + inv_rms * (dn - normed * inner)).astype(BF16)

    return pl.pallas_call(
        kernel,
        in_specs=here(9) + [pl.BlockSpec(memory_space=pl.ANY)] * len(first),
        out_specs=tuple(here(2)),
        out_shape=(shape(OWN, D), shape(8, 128, dtype=F32)),
        compiler_params=params(4),
        cost_estimate=cost(MIB, MIB),
        name="raw_last",
    )(mine, row, *gots, weight, inputs, cotangent, gain, *first)


def body(inputs, cotangent, segment_ids, norm_gain, w_in, w_out):
    dp = lax.axis_index("dp")
    y_lo, z = lax.div(dp, 8), lax.rem(dp, 8)
    spot = jnp.stack([y_lo, z])
    packed = pack(spot, inputs, cotangent, segment_ids, norm_gain)

    row = jnp.concatenate([packed] + [send(packed, first_axis(-o)) for o in OFFSETS[1:]], axis=0)
    w_in = lax.dynamic_slice_in_dim(w_in, y_lo * HID, HID, 1)
    w_out = lax.dynamic_slice_in_dim(w_out, y_lo * HID, HID, 0)
    plus, minus = send(row, second_axis(-1)), send(row, second_axis(1))
    swapped = send(copied(row, w_in, w_out), other_core)
    parts = [chunk(0, [row, swapped], w_in, w_out)]
    plus, minus = after([plus, minus], parts[0][1])
    relayed = [
        send(part, second_axis(o)) for part, o in zip(relay_halves(plus, minus), (-1, 1))
    ]
    parts.append(chunk(1, [plus, send(plus, other_core)], w_in, w_out))
    swapped = send(minus, other_core)
    parts.append(chunk(2, [minus, swapped], w_in, w_out, parts[1][1]))
    relayed = after(relayed, parts[2][1])
    parts.append(chunk(3, [*relayed, *(send(r, other_core) for r in relayed)], w_in, w_out))
    lefts, labs, rights, mine, theirs = zip(*parts)

    weight, up, down, theirs_all = far_call(spot, labs, lefts, rights, theirs)
    up_got, down_got = send(up, along_z(1)), send(down, along_z(-1))
    raw_got = send(theirs_all, other_core)
    raws = [raw for pair in zip(mine, theirs) for raw in pair]
    gain = gain_call(weight, lefts, raws)
    gain_got = send(gain, other_core)
    near = terms_call("near_terms", [(3, -3)], spot, weight, lefts, rights, gain)
    gain = gain + gain_got
    gain = gain + send(gain, xor_z(1))
    keep, *blocks = raw_first(mine, raw_got, gain, near)
    gots = [send(blocks[j], second_axis(OFFSETS[j + 1])) for j in (2, 0, 1)]

    up, down = ring_call(1, 0, near, up_got, down_got, *blocks)
    up_got, down_got = send(up, along_z(1)), send(down, along_z(-1))
    middle = terms_call("middle_terms", [(2, -2)], spot, weight, lefts, rights, up)

    up, down = ring_call(2, 0, middle, up_got, down_got, *gots)
    up_got, down_got = send(up, along_z(1)), send(down, along_z(-1))
    rest = terms_call("rest_terms", [(1, -1), (0,)], spot, weight, lefts, rights, up)
    own, row_sum, *blocks = raw_second(keep, gain, gots, up, down)
    gots = [send(blocks[j], first_axis(OFFSETS[j + 1])) for j in (2, 0, 1)]

    up, down = ring_call(3, 0, rest, up_got, down_got, *gots)
    up_got, down_got = send(up, along_z(1)), send(down, along_z(-1))
    input_grad, gain_grad = raw_last(
        own, row_sum, gots, weight, inputs, cotangent, norm_gain, up, down
    )
    gain_grad = gain_grad + sum(send(gain_grad, xor_z(o)) for o in (2, 4, 6))

    give = ring_last(1, spot, 2, rest, up_got, down_got, gain_grad)
    sums = ring_last(0, spot, 2, rest, up_got, down_got, give)
    outs = place(0, spot, sums, give)
    w_out_grad, w_in_grad = place(1, spot, send(give, partner_y), *outs)
    return (input_grad, w_in_grad, w_out_grad.T, gain_grad.reshape(D))


def solution(mesh):
    in_specs = (
        P(("dp", "mp"), None),
        P(("dp", "mp"), None),
        P("dp", "mp"),
        P(),
        P(None, "mp"),
        P("mp", None),
    )
    out_specs = (P(("dp", "mp"), None), P("dp", "mp"), P("mp", "dp"), P())
    return jax.shard_map(body, mesh=mesh, in_specs=in_specs, out_specs=out_specs, check_vma=False)
```

```python
import functools
import math

import jax
import jax.numpy as jnp
from jax import lax
from jax.experimental import pallas as pl
from jax.experimental.pallas import tpu as pltpu
from jax.sharding import PartitionSpec as P

TOK_GROUP = 640
SEGS = 8
OWN = 40
ROW = 4 * OWN
CHUNK = 2 * ROW
PLANE = 4 * CHUNK
D = 1024
HID = 1024
PACK = 2 * D + 128
AXES = ("dp", "mp")
OFFSETS = (0, 1, -1, 2)
MIB = 1024 * 1024

GELU_C = 0.7978845608
GELU_A = 0.044715
F32, BF16 = jnp.float32, jnp.bfloat16


def coords(index):
    dp, mp = divmod(index, 16)
    return ((mp // 2) % 4, (mp // 8) * 2 + dp // 8, dp % 8, mp % 2)


def index_of(x, y, z, c):
    x, y, z = x % 4, y % 4, z % 8
    return ((y % 2) * 8 + z) * 16 + ((y // 2) * 4 + x) * 2 + c


def send(value, move):
    pairs = [(i, index_of(*move(*coords(i)))) for i in range(256)]
    return lax.ppermute(value, AXES, pairs)


def first_axis(o):
    return lambda x, y, z, c: (x + o, y, z, c) if c == 0 else (x, y + o, z, c)


def second_axis(o):
    return lambda x, y, z, c: (x, y + o, z, c) if c == 0 else (x + o, y, z, c)


def other_core(x, y, z, c):
    return (x, y, z, 1 - c)


def partner_y(x, y, z, c):
    return (x, y ^ 1, z, c)


def along_z(o):
    return lambda x, y, z, c: (x, y, z + o, c)


def xor_z(o):
    return lambda x, y, z, c: (x, y, z ^ o, c)


def params(mib):
    return pltpu.CompilerParams(vmem_limit_bytes=mib * MIB)


def cost(flops, moved, trans=0):
    return pl.CostEstimate(flops=flops, bytes_accessed=moved, transcendentals=trans)


def here(count):
    return [pl.BlockSpec(memory_space=pltpu.VMEM)] * count


def scalar():
    return pl.BlockSpec(memory_space=pltpu.SMEM)


def shape(*dims, dtype=BF16):
    return jax.ShapeDtypeStruct(dims, dtype)


def pack_kernel(spot_ref, x_hbm, cot_hbm, ids_hbm, gain_hbm, out_ref, x_ref, cot_ref, ids_ref, gain_ref, sems):
    copies = [
        pltpu.make_async_copy(src, dst, sems.at[k])
        for k, (src, dst) in enumerate(
            [(x_hbm, x_ref), (cot_hbm, cot_ref), (ids_hbm, ids_ref), (gain_hbm, gain_ref)]
        )
    ]
    for copy in copies:
        copy.start()
    for copy in copies:
        copy.wait()
    floats = x_ref[...].astype(F32)
    inv_rms = lax.rsqrt(jnp.mean(floats * floats, axis=-1, keepdims=True) + 1e-06)
    normed = floats * inv_rms
    out_ref[:, :D] = cot_ref[...]
    out_ref[:, D : 2 * D] = (normed * gain_ref[...].astype(F32).reshape(1, D)).astype(BF16)
    ids = jnp.broadcast_to((ids_ref[...] + SEGS * spot_ref[0]).astype(F32), (OWN, OWN))
    along = lax.broadcasted_iota(jnp.int32, (OWN, OWN), 0)
    across = lax.broadcasted_iota(jnp.int32, (OWN, OWN), 1)
    label = jnp.sum(jnp.where(along == across, ids, 0.0), axis=1, keepdims=True)
    out_ref[:, 2 * D :] = jnp.broadcast_to(label, (OWN, 128)).astype(BF16)


def pack(spot, inputs, cotangent, ids, gain):
    inputs_in_hbm = [
        pltpu.with_memory_space_constraint(a, pltpu.HBM) for a in (inputs, cotangent, ids, gain)
    ]
    return pl.pallas_call(
        pack_kernel,
        in_specs=[pl.BlockSpec(memory_space=pltpu.SMEM)]
        + [pl.BlockSpec(memory_space=pltpu.HBM)] * 4,
        out_shape=jax.ShapeDtypeStruct((OWN, PACK), BF16),
        scratch_shapes=[
            pltpu.VMEM((OWN, D), BF16),
            pltpu.VMEM((OWN, D), BF16),
            pltpu.VMEM((1, OWN), jnp.int32),
            pltpu.VMEM((D,), BF16),
            pltpu.SemaphoreType.DMA((4,)),
        ],
        compiler_params=params(4),
        cost_estimate=cost(OWN * D * 8, 4 * OWN * D * 2),
        name="pack_rows",
    )(spot, *inputs_in_hbm)


def nothing(*refs):
    pass


def after(values, *first):
    anywhere = pl.BlockSpec(memory_space=pl.ANY)
    return pl.pallas_call(
        nothing,
        in_specs=[anywhere] * (len(values) + len(first)),
        out_specs=[anywhere] * len(values),
        out_shape=[jax.ShapeDtypeStruct(v.shape, v.dtype) for v in values],
        input_output_aliases={k: k for k in range(len(values))},
        compiler_params=params(1),
        cost_estimate=cost(0, 0),
        name="after",
    )(*values, *first)


def copied(value, *first):
    def kernel(value_ref, *refs):
        refs[-1][...] = value_ref[...]

    return pl.pallas_call(
        kernel,
        in_specs=here(1) + [pl.BlockSpec(memory_space=pl.ANY)] * len(first),
        out_specs=here(1)[0],
        out_shape=shape(*value.shape),
        compiler_params=params(2),
        cost_estimate=cost(0, MIB),
        name="copied",
    )(value, *first)


def relay_halves(plus, minus, *first):
    def kernel(plus_ref, minus_ref, *refs):
        refs[-2][...] = plus_ref[: ROW // 2, :]
        refs[-1][...] = minus_ref[ROW // 2 :, :]

    return pl.pallas_call(
        kernel,
        in_specs=here(2) + [pl.BlockSpec(memory_space=pl.ANY)] * len(first),
        out_specs=tuple(here(2)),
        out_shape=(shape(ROW // 2, PACK),) * 2,
        compiler_params=params(2),
        cost_estimate=cost(0, MIB),
        name="relay_halves",
    )(plus, minus, *first)


STEPS = 1
WIDTH = HID // STEPS


def chunk_kernel(count, *refs):
    srcs, (w_in_ref, w_out_ref) = refs[:count], refs[count : count + 2]
    left_ref, lab_ref, right_ref, mine_ref, theirs_ref, acc = refs[-6:]
    size = CHUNK // count
    for k, src in enumerate(srcs):
        rows = slice(k * size, (k + 1) * size)
        left_ref[rows, :] = src[:, : 2 * D]
        lab_ref[rows, :] = src[:, 2 * D :]
    for step in range(STEPS):
        cols = slice(step * WIDTH, (step + 1) * WIDTH)
        p = jnp.dot(left_ref[:, D:], w_in_ref[:, cols], preferred_element_type=F32)
        g = lax.dot_general(
            left_ref[:, :D], w_out_ref[cols, :], (((1,), (1,)), ((), ())), preferred_element_type=F32
        )
        p2 = p * p
        h = 0.5 * jnp.tanh(p * (GELU_C + (GELU_C * GELU_A) * p2)) + 0.5
        q = p * (2.0 * GELU_C + (6.0 * GELU_C * GELU_A) * p2)
        right_ref[:, cols] = (p * h).astype(BF16)
        pre_grad = (g * (h * (1.0 + (q - q * h)))).astype(BF16)
        right_ref[:, HID + step * WIDTH : HID + (step + 1) * WIDTH] = pre_grad
        raw = lax.dot_general(
            pre_grad, w_in_ref[:, cols], (((1,), (1,)), ((), ())), preferred_element_type=F32
        )
        if step > 0:
            raw = raw + acc[...]
        if step < STEPS - 1:
            acc[...] = raw
        else:
            mine_ref[...] = raw[:ROW].astype(BF16)
            theirs_ref[...] = raw[ROW:].astype(BF16)


def chunk(j, srcs, w_in, w_out, *first):
    shapes = [(CHUNK, 2 * D), (CHUNK, 128), (CHUNK, 2 * HID), (ROW, D), (ROW, D)]
    return pl.pallas_call(
        functools.partial(chunk_kernel, len(srcs)),
        in_specs=here(len(srcs) + 2) + [pl.BlockSpec(memory_space=pl.ANY)] * len(first),
        out_specs=here(5),
        scratch_shapes=[pltpu.VMEM((CHUNK, D), F32)],
        out_shape=[shape(*s) for s in shapes],
        compiler_params=params(14),
        cost_estimate=cost(*((10**8, MIB) if j == 0 else (6 * CHUNK * D * HID, 9 * MIB, CHUNK * HID))),
        name="chunk_%d" % j,
    )(*srcs, w_in, w_out, *first)


def token_weights(labels):
    labels = labels.astype(F32)
    lanes = lax.broadcasted_iota(jnp.int32, (PLANE, 128), 1).astype(F32)
    onehot = jnp.where(labels == lanes, 1.0, 0.0)
    counts = jnp.sum(onehot, axis=0, keepdims=True)
    lane = lax.broadcasted_iota(jnp.int32, (1, 128), 1)
    none = (lane == SEGS - 1) | (lane == 2 * SEGS - 1) | (counts == 0.0)
    table = jnp.where(none, 0.0, jnp.sqrt(TOK_GROUP / (SEGS * jnp.maximum(counts, 1.0))))
    return jnp.sum(onehot * table, axis=1, keepdims=True)


GRAD_SCALE = 1.0 / math.sqrt(TOK_GROUP * 16)


RIDE = 16


def fold(row):
    return jnp.concatenate([row[:, k * 128 : (k + 1) * 128] for k in range(8)], axis=0)


def unfold(block):
    return jnp.concatenate([block[k : k + 1, :] for k in range(8)], axis=1)


def gain_call(weight, lefts, raws, *first):
    def kernel(w_ref, *refs):
        lefts, raws, gain_ref = refs[:4], refs[4:12], refs[-1]
        total = jnp.zeros((1, D), F32)
        for k, raw in enumerate(raws):
            rows = slice((k % 2) * ROW, (k % 2 + 1) * ROW)
            w = w_ref[k * ROW : (k + 1) * ROW, :1]
            term = lefts[k // 2][rows, D:].astype(F32) * raw[...].astype(F32) * w
            total = total + jnp.sum(term, axis=0, keepdims=True)
        gain_ref[...] = fold(total)

    anywhere = pl.BlockSpec(memory_space=pl.ANY)
    return pl.pallas_call(
        kernel,
        in_specs=here(13) + [anywhere] * len(first),
        out_shape=shape(8, 128, dtype=F32),
        compiler_params=params(8),
        cost_estimate=cost(4 * PLANE * D, 8 * MIB),
        name="gain_term",
    )(weight, *lefts, *raws, *first)


def term_block(array, offsets, z, weight, lefts, rights):
    low = (lax.broadcasted_iota(jnp.int32, (PLANE, 128), 1) < 64).astype(jnp.int32)
    blocks = []
    for offset in offsets:
        to = lax.rem(z + offset + 8, 8)
        odd = lax.rem(to, 2)
        start = array * D + (to // 2) * 128
        moved, kept = (
            jnp.concatenate([ref[:, pl.ds(pl.multiple_of(at, 128), 128)] for ref in lefts], axis=0)
            for at in (start + (1 - odd) * (D // 2), start + odd * (D // 2))
        )
        moved = pltpu.roll(moved.astype(F32), 64, 1)
        blocks.append((jnp.where(low == odd, moved, kept.astype(F32)) * weight).astype(BF16))
    left = jnp.concatenate(blocks, axis=1)
    right = jnp.concatenate([ref[:, array * HID : (array + 1) * HID] for ref in rights], axis=0)
    total = lax.dot_general(left, right, (((0,), (0,)), ((), ())), preferred_element_type=F32)
    return (total * GRAD_SCALE).astype(BF16)


def far_call(spot, labs, lefts, rights, theirs):
    def kernel(spot_ref, *refs):
        labs, lefts, rights, theirs = refs[:4], refs[4:8], refs[8:12], refs[12:16]
        weight_ref, up_ref, down_ref, theirs_ref = refs[16:]
        weights = token_weights(jnp.concatenate([lab[...] for lab in labs], axis=0))
        weight_ref[...] = jnp.broadcast_to(weights, (PLANE, 128))
        for array, ref in enumerate((up_ref, down_ref)):
            block = term_block(array, (4,), spot_ref[1], weight_ref[...], lefts, rights)
            ref[...] = block.reshape(2, 64, HID)
        for j, raw in enumerate(theirs):
            theirs_ref[j * ROW : (j + 1) * ROW, :] = raw[...]

    return pl.pallas_call(
        kernel,
        in_specs=[scalar()] + here(16),
        out_specs=tuple(here(4)),
        out_shape=(
            shape(PLANE, 128, dtype=F32),
            shape(2, 64, HID),
            shape(2, 64, HID),
            shape(TOK_GROUP, D),
        ),
        compiler_params=params(12),
        cost_estimate=cost(PLANE * D * HID, 8 * MIB),
        name="far_terms",
    )(spot, *labs, *lefts, *rights, *theirs)


def terms_call(name, groups, spot, weight, lefts, rights, *first):
    count = sum(len(group) for group in groups)

    def kernel(spot_ref, weight_ref, *refs):
        lefts, rights, out_ref = refs[:4], refs[4:8], refs[-1]
        at = 0
        for group in groups:
            for array in range(2):
                block = term_block(array, group, spot_ref[1], weight_ref[...], lefts, rights)
                block = block.reshape(len(group), 2, 64, HID)
                for k in range(len(group)):
                    out_ref[at + k, array] = block[k]
            at += len(group)

    return pl.pallas_call(
        kernel,
        in_specs=[scalar()] + here(9) + [pl.BlockSpec(memory_space=pl.ANY)] * len(first),
        out_specs=here(1)[0],
        out_shape=shape(count, 2, 2, 64, HID),
        compiler_params=params(12),
        cost_estimate=cost(count * PLANE * 512 * HID, 8 * MIB),
        name=name,
    )(spot, weight, *lefts, *rights, *first)


def add(*terms):
    return sum(t.astype(F32) for t in terms).astype(BF16)


def ring_call(step, at, terms, plus, minus, *first):
    def kernel(terms_ref, plus_ref, minus_ref, *refs):
        up_ref, down_ref = refs[-2:]
        if step == 1:
            up_ref[0] = add(plus_ref[...], terms_ref[at, 0])
            up_ref[1] = terms_ref[at, 1]
            down_ref[0] = terms_ref[at + 1, 0]
            down_ref[1] = add(minus_ref[...], terms_ref[at + 1, 1])
        else:
            for array in range(2):
                up_ref[array] = add(plus_ref[array], terms_ref[at, array])
                down_ref[array] = add(minus_ref[array], terms_ref[at + 1, array])

    anywhere = pl.BlockSpec(memory_space=pl.ANY)
    return pl.pallas_call(
        kernel,
        in_specs=here(3) + [anywhere] * len(first),
        out_specs=tuple(here(2)),
        out_shape=(shape(2, 2, 64, HID),) * 2,
        compiler_params=params(4),
        cost_estimate=cost(4 * MIB, 4 * MIB),
        name="ring_%d" % step,
    )(terms, plus, minus, *first)


def ring_last(other, spot, at, terms, plus, minus, *first):
    def kernel(spot_ref, terms_ref, plus_ref, minus_ref, *refs):
        y = spot_ref[0] if other == 0 else 1 - spot_ref[0]
        for array in range(2):
            refs[-1][array] = add(terms_ref[at, array, y], plus_ref[array, y], minus_ref[array, y])

    anywhere = pl.BlockSpec(memory_space=pl.ANY)
    return pl.pallas_call(
        kernel,
        in_specs=[scalar()] + here(3) + [anywhere] * len(first),
        out_specs=here(1)[0],
        out_shape=shape(2, 64, HID),
        compiler_params=params(4),
        cost_estimate=cost(MIB, 2 * MIB),
        name="ring_last_%d" % other,
    )(spot, terms, plus, minus, *first)


def place(other, spot, half, *outs):
    olds = outs if other else ()

    def kernel(spot_ref, half_ref, *refs):
        *_, first, second, sems = refs
        column = spot_ref[0] if other == 0 else 1 - spot_ref[0]
        cols = pl.ds(pl.multiple_of(column * HID, HID), HID)
        copies = [
            pltpu.make_async_copy(half_ref.at[array], out.at[:, cols], sems.at[array])
            for array, out in enumerate((first, second))
        ]
        for copy in copies:
            copy.start()
        for copy in copies:
            copy.wait()

    anywhere = [pl.BlockSpec(memory_space=pl.ANY)]
    return pl.pallas_call(
        kernel,
        in_specs=[scalar()] + here(1) + anywhere * len(outs),
        out_specs=(pl.BlockSpec(memory_space=pltpu.HBM),) * 2,
        out_shape=(pltpu.HBM((64, 2 * HID), BF16),) * 2,
        scratch_shapes=[pltpu.SemaphoreType.DMA((2,))],
        input_output_aliases={2 + k: k for k in range(len(olds))},
        compiler_params=params(4),
        cost_estimate=cost(MIB, MIB),
        name="place_%d" % other,
    )(spot, half, *outs)


def ride_rows(total):
    high = total.astype(BF16).astype(F32)
    rows = lax.broadcasted_iota(jnp.int32, (RIDE, D), 0)
    return jnp.where(rows == 0, high, jnp.where(rows == 1, total - high, 0.0)).astype(BF16)


def ride_sum(rows):
    return jnp.sum(rows.astype(F32), axis=0, keepdims=True)


def raw_first(mine, got, gain, *first):
    def kernel(*refs):
        mines, got_ref, gain_ref = refs[:4], refs[4], refs[5]
        keep_ref, *sends = refs[-4:]
        keep_ref[...] = mines[0][...].astype(F32) + got_ref[:ROW, :].astype(F32)
        ride = ride_rows(unfold(gain_ref[...]))
        for j in range(1, 4):
            sends[j - 1][:ROW, :] = add(mines[j][...], got_ref[j * ROW : (j + 1) * ROW, :])
            sends[j - 1][ROW:, :] = ride

    anywhere = pl.BlockSpec(memory_space=pl.ANY)
    return pl.pallas_call(
        kernel,
        in_specs=here(6) + [anywhere] * len(first),
        out_specs=tuple(here(4)),
        out_shape=(shape(ROW, D, dtype=F32),) + (shape(ROW + RIDE, D),) * 3,
        compiler_params=params(4),
        cost_estimate=cost(2 * MIB, 4 * MIB),
        name="raw_first",
    )(*mine, got, gain, *first)


def raw_second(keep, gain, gots, *first):
    def kernel(keep_ref, gain_ref, *refs):
        gots = refs[:3]
        mine_ref, total_ref, *sends = refs[-5:]
        total = keep_ref[...]
        row = ride_sum(ride_rows(unfold(gain_ref[...])))
        for got in gots:
            total = total + got[:ROW, :].astype(F32)
            row = row + ride_sum(got[ROW:, :])
        ride = ride_rows(row)
        mine_ref[...] = total[:OWN]
        total_ref[...] = jnp.broadcast_to(ride_sum(ride), (8, D))
        for j in range(1, 4):
            block = jnp.concatenate([total[j * OWN : (j + 1) * OWN], jnp.zeros((8, D), F32)], axis=0)
            sends[j - 1][: OWN + 8, :] = block.astype(BF16)
            sends[j - 1][OWN + 8 :, :] = ride

    anywhere = pl.BlockSpec(memory_space=pl.ANY)
    return pl.pallas_call(
        kernel,
        in_specs=here(5) + [anywhere] * len(first),
        out_specs=tuple(here(5)),
        out_shape=(shape(OWN, D, dtype=F32), shape(8, D, dtype=F32))
        + (shape(OWN + 8 + RIDE, D),) * 3,
        compiler_params=params(6),
        cost_estimate=cost(2 * MIB, 2 * MIB),
        name="raw_second",
    )(keep, gain, *gots, *first)


def raw_last(mine, row, gots, weight, inputs, cotangent, gain, *first):
    def kernel(mine_ref, row_ref, *refs):
        gots, (w_ref, x_ref, cot_ref, gain_ref), (grad_ref, gain_out) = refs[:3], refs[3:7], refs[-2:]
        raw, row = mine_ref[...], row_ref[:1, :]
        for got in gots:
            raw = raw + got[: OWN + 8, :].astype(F32)[:OWN]
            row = row + ride_sum(got[OWN + 8 :, :])
        gain = gain_ref[...].astype(F32).reshape(1, D)
        gain_out[...] = fold(row / gain)
        w = w_ref[:OWN, :1]
        floats = x_ref[...].astype(F32)
        inv_rms = lax.rsqrt(jnp.mean(floats * floats, axis=-1, keepdims=True) + 1e-06)
        normed = floats * inv_rms
        dn = raw * w * gain
        inner = jnp.mean(dn * normed, axis=-1, keepdims=True)
        ge = (cot_ref[...].astype(F32) * w).astype(BF16).astype(F32)
        grad_ref[...] = (ge + inv_rms * (dn - normed * inner)).astype(BF16)

    return pl.pallas_call(
        kernel,
        in_specs=here(9) + [pl.BlockSpec(memory_space=pl.ANY)] * len(first),
        out_specs=tuple(here(2)),
        out_shape=(shape(OWN, D), shape(8, 128, dtype=F32)),
        compiler_params=params(4),
        cost_estimate=cost(MIB, MIB),
        name="raw_last",
    )(mine, row, *gots, weight, inputs, cotangent, gain, *first)


def body(inputs, cotangent, segment_ids, norm_gain, w_in, w_out):
    dp = lax.axis_index("dp")
    y_lo, z = lax.div(dp, 8), lax.rem(dp, 8)
    spot = jnp.stack([y_lo, z])
    packed = pack(spot, inputs, cotangent, segment_ids, norm_gain)

    row = jnp.concatenate([packed] + [send(packed, first_axis(-o)) for o in OFFSETS[1:]], axis=0)
    w_in = lax.dynamic_slice_in_dim(w_in, y_lo * HID, HID, 1)
    w_out = lax.dynamic_slice_in_dim(w_out, y_lo * HID, HID, 0)
    plus, minus = send(row, second_axis(-1)), send(row, second_axis(1))
    swapped = send(copied(row, w_in, w_out), other_core)
    parts = [chunk(0, [row, swapped], w_in, w_out)]
    plus, minus = after([plus, minus], parts[0][1])
    relayed = [
        send(part, second_axis(o)) for part, o in zip(relay_halves(plus, minus), (-1, 1))
    ]
    parts.append(chunk(1, [plus, minus], w_in, w_out))
    swapped = [send(plus, other_core), send(minus, other_core)]
    parts.append(chunk(2, swapped, w_in, w_out, parts[1][1]))
    relayed = after(relayed, parts[2][1])
    parts.append(chunk(3, [*relayed, *(send(r, other_core) for r in relayed)], w_in, w_out))
    lefts, labs, rights, first, second = zip(*parts)
    mine = (first[0], first[1], second[1], first[3])
    theirs = (second[0], first[2], second[2], second[3])

    weight, up, down, theirs_all = far_call(spot, labs, lefts, rights, theirs)
    up_got, down_got = send(up, along_z(1)), send(down, along_z(-1))
    raw_got = send(theirs_all, other_core)
    raws = [raw for pair in zip(first, second) for raw in pair]
    gain = gain_call(weight, lefts, raws)
    gain_got = send(gain, other_core)
    near = terms_call("near_terms", [(3, -3)], spot, weight, lefts, rights, gain)
    gain = gain + gain_got
    gain = gain + send(gain, xor_z(1))
    keep, *blocks = raw_first(mine, raw_got, gain, near)
    gots = [send(blocks[j], second_axis(OFFSETS[j + 1])) for j in (2, 0, 1)]

    up, down = ring_call(1, 0, near, up_got, down_got, *blocks)
    up_got, down_got = send(up, along_z(1)), send(down, along_z(-1))
    middle = terms_call("middle_terms", [(2, -2)], spot, weight, lefts, rights, up)

    up, down = ring_call(2, 0, middle, up_got, down_got, *gots)
    up_got, down_got = send(up, along_z(1)), send(down, along_z(-1))
    rest = terms_call("rest_terms", [(1, -1), (0,)], spot, weight, lefts, rights, up)
    own, row_sum, *blocks = raw_second(keep, gain, gots, up, down)
    gots = [send(blocks[j], first_axis(OFFSETS[j + 1])) for j in (2, 0, 1)]

    up, down = ring_call(3, 0, rest, up_got, down_got, *gots)
    up_got, down_got = send(up, along_z(1)), send(down, along_z(-1))
    input_grad, gain_grad = raw_last(
        own, row_sum, gots, weight, inputs, cotangent, norm_gain, up, down
    )
    gain_grad = gain_grad + sum(send(gain_grad, xor_z(o)) for o in (2, 4, 6))

    give = ring_last(1, spot, 2, rest, up_got, down_got, gain_grad)
    sums = ring_last(0, spot, 2, rest, up_got, down_got, give)
    outs = place(0, spot, sums, give)
    w_out_grad, w_in_grad = place(1, spot, send(give, partner_y), *outs)
    return (input_grad, w_in_grad, w_out_grad.T, gain_grad.reshape(D))


def solution(mesh):
    in_specs = (
        P(("dp", "mp"), None),
        P(("dp", "mp"), None),
        P("dp", "mp"),
        P(),
        P(None, "mp"),
        P("mp", None),
    )
    out_specs = (P(("dp", "mp"), None), P("dp", "mp"), P("mp", "dp"), P())
    return jax.shard_map(body, mesh=mesh, in_specs=in_specs, out_specs=out_specs, check_vma=False)
```
